1024 devices in a mesh: gx: 4 (over z_hi), gy: 8 (over z_lo, core), gz: 32 (over x, y).
Axes of the slice: x: 4, y: 8, z: 16 (z_hi: 4, z_lo: 4; z = z_hi * 4 + z_lo), core: 2. Of those that a mesh axis runs over, the one named last changes fastest.
Arguments:
- orbitals: float32 [4, 128, 64, 512], P(None, 'gz', 'gy', 'gx'), may hold values from -18 to 18
- potential: float32 [128, 64, 512], P('gz', 'gy', 'gx'), may hold values from -6 to 6
- block_atom: int32 [32, 8, 4, 16], P('gz', 'gy', 'gx'), may hold values from 0 to 3071, as said below
- block_points: int32 [32, 8, 4, 16, 128], P('gz', 'gy', 'gx'), may hold values from 0 to 4095
- block_count: int32 [32, 8, 4], P('gz', 'gy', 'gx'), may hold values from 1 to 16, as said below
- projector_values: float32 [32, 8, 4, 16, 8, 128], P('gz', 'gy', 'gx'), may hold values from -0.5 to 0.5
- coupling: float32 [2, 8, 8], replicated, may hold values from -3 to 3, as said below
Outputs:
- hamiltonian_image: float32 [4, 128, 64, 512], P(None, 'gz', 'gy', 'gx')
- residual: float32 [4, 128, 64, 512], P(None, 'gz', 'gy', 'gx')
The draws below stay inside these ranges and needn't reach their ends.
Inputs may be any that keep to these rules, and one draw needn't show every extreme that they name: `block_atom`: atoms are numbered by owning box, boxes numbered z slowest, then y, then x: atom a is owned by box a // 3. The owner of a slot's atom lies at most one box away from the slot's box along each of the three directions, the boxes wrapping around. A box's slots from block_count on are padding. `coupling`: Symmetric.
All inputs are finite; a program needn't handle non-finite values.
Results may differ from the reference program's by a relative error of at most 0.00005.
Values sent between devices are 32-bit elements; how exact they have to be, the bound alone decides.
A program may use at most 64 MiB of HBM per device.

```python
import jax
import jax.numpy as jnp
from jax import lax

BX = 128
BY = 8
BZ = 4
ATOM_DEV = 3
PBLK = 16
ORB = 4
NPROJ = 8
BOXES_X = 4
BOXES_Y = 8
BOXES_Z = 32
NX = 512
NY = 64
NZ = 128
NPOINTS = 4194304
ATOMS = 3072


def draw_orbitals(key, part):
    key = jax.random.fold_in(key, 11)
    depth = (jnp.arange(NZ, dtype=jnp.float32) + 0.5) / NZ
    base = jnp.clip(jax.random.normal(key, (ORB, NZ, NY, NX), jnp.float32), -6.0, 6.0)
    scale = 3.0 ** depth
    return base * scale[None, :, None, None]


def draw_block_atom(key, part):
    key = jax.random.fold_in(key, 31)
    shape = (BOXES_Z, BOXES_Y, BOXES_X, PBLK)
    key_z, key_y, key_x, key_k = jax.random.split(key, 4)
    cell_z = lax.broadcasted_iota(jnp.int32, shape, 0)
    cell_y = lax.broadcasted_iota(jnp.int32, shape, 1)
    cell_x = lax.broadcasted_iota(jnp.int32, shape, 2)
    owner_z = jnp.mod(cell_z + jax.random.randint(key_z, shape, -1, 2), BOXES_Z)
    owner_y = jnp.mod(cell_y + jax.random.randint(key_y, shape, -1, 2), BOXES_Y)
    owner_x = jnp.mod(cell_x + jax.random.randint(key_x, shape, -1, 2), BOXES_X)
    within = jax.random.randint(key_k, shape, 0, ATOM_DEV)
    atom_ids = ((owner_z * BOXES_Y + owner_y) * BOXES_X + owner_x) * ATOM_DEV + within
    flat_ids = atom_ids.reshape(-1)
    flat_ids = flat_ids.at[0].set(ATOMS - 1).at[1].set(0)
    return flat_ids.reshape(shape).astype(jnp.int32)


def draw_block_count(key, part):
    key = jax.random.fold_in(key, 47)
    shape = (BOXES_Z, BOXES_Y, BOXES_X)
    key_base, key_heavy, key_place = jax.random.split(key, 3)
    counts = jax.random.randint(key_base, shape, max(1, PBLK // 8), PBLK // 2 + 1)
    heavy = jax.random.randint(key_heavy, shape, 0, 8) == 0
    counts = jnp.where(heavy, PBLK, counts).reshape(-1)
    place = jax.random.randint(key_place, (), 0, BOXES_Z * BOXES_Y * BOXES_X)
    marker = jnp.arange(BOXES_Z * BOXES_Y * BOXES_X, dtype=jnp.int32) == place
    counts = jnp.where(marker, PBLK, counts)
    return counts.reshape(shape).astype(jnp.int32)


def draw_coupling(key, part):
    key = jax.random.fold_in(key, 23)
    key_off, key_diag = jax.random.split(key)
    rough = jnp.clip(jax.random.normal(key_off, (2, NPROJ, NPROJ), jnp.float32) * 0.4, -1.0, 1.0)
    symmetric = 0.5 * (rough + jnp.transpose(rough, (0, 2, 1)))
    diagonal = jax.random.uniform(key_diag, (2, NPROJ), jnp.float32, 1.5, 3.0)
    identity = jnp.eye(NPROJ, dtype=jnp.float32)[None]
    return symmetric * (1.0 - identity) + diagonal[:, :, None] * identity


def touch_ends(result, stream_key, low, largest):
    shape = result.shape
    spot = [jax.random.randint(jax.random.fold_in(stream_key, axis), (), 0, shape[axis]) for axis in range(len(shape))]
    result = result.at[tuple(spot)].set(low)
    longest = shape.index(max(shape))
    spot[longest] = (spot[longest] + 1) % shape[longest]
    return result.at[tuple(spot)].set(largest)


def shard_levels(rng, extent, cuts, low, top_value):
    gain = 1.0
    for dim, parts in cuts:
        draws = jax.random.uniform(jax.random.fold_in(jax.random.fold_in(rng, 6), dim), (parts,), jnp.float32, low / len(cuts), top_value / len(cuts))
        gain = gain * jnp.repeat(jnp.exp(draws), extent[dim] // parts).reshape((-1,) + (1,) * (len(extent) - 1 - dim))
    return gain


def centred(stream_key, extent, scale, reach, shards=(), held_as=jnp.bfloat16):
    result = scale * jax.random.normal(stream_key, extent, jnp.float32)
    if shards:
        result = result * shard_levels(stream_key, extent, shards, -0.22, 0.18)
    return jnp.clip(result, -reach, reach).astype(held_as)


def setup_inputs(seed: int = 0) -> dict:
    key_of = jax.random.split(jax.random.key(seed), 8)
    return {
        "orbitals": draw_orbitals(jax.random.fold_in(key_of[7], 71), 0),
        "potential": centred(key_of[1], (NZ, NY, NX), 1.0, 6.0, ((0, 32), (1, 8), (2, 4)), jnp.float32),
        "block_atom": draw_block_atom(jax.random.fold_in(key_of[7], 71), 0),
        "block_points": touch_ends(jax.random.randint(key_of[3], (BOXES_Z, BOXES_Y, BOXES_X, PBLK, 128), 0, BZ * BY * BX), jax.random.fold_in(key_of[3], 1), 0, (BZ * BY * BX) - 1).astype(jnp.int32),
        "block_count": draw_block_count(jax.random.fold_in(key_of[7], 71), 0),
        "projector_values": centred(key_of[5], (BOXES_Z, BOXES_Y, BOXES_X, PBLK, NPROJ, 128), 128 ** -0.5, 0.5, ((0, 32), (1, 8), (2, 4)), jnp.float32),
        "coupling": draw_coupling(jax.random.fold_in(key_of[7], 71), 0),
    }


STENCIL = (-205.0 / 72.0, 8.0 / 5.0, -1.0 / 5.0, 8.0 / 315.0, -1.0 / 560.0)
HIGH = lax.Precision.HIGHEST


def kinetic_whole(fields):
    laplace = 3.0 * STENCIL[0] * fields
    for offset in range(1, 5):
        for axis_pos in (1, 2, 3):
            laplace = laplace + STENCIL[offset] * (jnp.roll(fields, offset, axis_pos) + jnp.roll(fields, -offset, axis_pos))
    return -0.5 * laplace


def coupling_for(coupling, atom_ids):
    oxygen = (atom_ids % 3 == 0)[:, None, None]
    return jnp.where(oxygen, coupling[0][None], coupling[1][None])


def reference(orbitals, potential, block_atom, block_points, block_count, projector_values, coupling):
    box_count = BOXES_Z * BOXES_Y * BOXES_X
    box_points = BZ * BY * BX
    box_fields = orbitals.reshape(ORB, BOXES_Z, BZ, BOXES_Y, BY, BOXES_X, BX).transpose(1, 3, 5, 0, 2, 4, 6).reshape(box_count, ORB, box_points)
    points = block_points.reshape(box_count, PBLK, 128)
    beta_rows = projector_values.reshape(box_count, PBLK, NPROJ, 128)
    atom_ids = block_atom.reshape(box_count, PBLK)
    in_use = (jnp.arange(PBLK, dtype=jnp.int32)[None, :] < block_count.reshape(box_count, 1)).astype(jnp.float32)

    def gather_box(one_box, slot_points):
        return one_box[:, slot_points]

    gathered = jax.vmap(gather_box)(box_fields, points)
    partial_terms = jnp.einsum("ebpq,enbq->ebpn", beta_rows, gathered, precision=HIGH) * in_use[:, :, None, None]
    flat_atoms = atom_ids.reshape(-1)
    coefficients = jnp.zeros((ATOMS, NPROJ, ORB), jnp.float32).at[flat_atoms].add(partial_terms.reshape(-1, NPROJ, ORB))
    picked = coefficients[flat_atoms]
    applied = jnp.einsum("apq,aqn->apn", coupling_for(coupling, flat_atoms), picked, precision=HIGH).reshape(box_count, PBLK, NPROJ, ORB)
    values = jnp.einsum("ebpq,ebpn->enbq", beta_rows, applied, precision=HIGH) * in_use[:, None, :, None]

    def scatter_box(slot_points, slot_values):
        return jnp.zeros((ORB, box_points), jnp.float32).at[:, slot_points.reshape(-1)].add(slot_values.reshape(ORB, -1))

    projected_boxes = jax.vmap(scatter_box)(points, values)
    projected = projected_boxes.reshape(BOXES_Z, BOXES_Y, BOXES_X, ORB, BZ, BY, BX).transpose(3, 0, 4, 1, 5, 2, 6).reshape(orbitals.shape)
    image = kinetic_whole(orbitals) + potential[None] * orbitals + projected
    flat_orbitals = orbitals.reshape(ORB, -1)
    flat_image = image.reshape(ORB, -1)
    gram_matrix = jnp.dot(flat_orbitals, flat_image.T, precision=HIGH) / NPOINTS
    residual = image - jnp.dot(gram_matrix.T, flat_orbitals, precision=HIGH).reshape(orbitals.shape)
    return image, residual
```

```python
import jax
import jax.numpy as jnp
from jax import lax
from jax.experimental import pallas as pl
from jax.experimental.pallas import tpu as pltpu
from jax.sharding import PartitionSpec as P

MESH = pl.DeviceIdType.MESH
HIGH = lax.Precision.HIGHEST
SIZES = (4, 8, 32)
GRID_TOTAL = 4194304
STENCIL = (-205.0 / 72.0, 8.0 / 5.0, -1.0 / 5.0, 8.0 / 315.0, -1.0 / 560.0)
KIN = tuple(-0.5 * c for c in STENCIL)
DIRS = [(d % 3 - 1, d // 3 % 3 - 1, d // 9 - 1) for d in range(27)]
OTHERS = [d for d in range(27) if d != 13]
PAIRS = [(i, j) for j in range(4) for i in range(j + 1)]
HALOS = [(0, 0, 1), (0, 0, -1), (0, 1, 0), (0, -1, 0), (1, 0, 0), (-1, 0, 0)]


def here():
    return lax.axis_index("gx"), lax.axis_index("gy"), lax.axis_index("gz")


def at_offset(delta):
    return tuple(
        v if d % n == 0 else (v + (d % n)) & (n - 1) for v, d, n in zip(here(), delta, SIZES)
    )


PLANE = [(0, 0, d) for d in range(1, 32)]
COLUMN = [(dx, dy, 0) for dx in range(4) for dy in range(8) if (dx, dy) != (0, 0)]


def all_partners():
    wanted = [DIRS[d] for d in OTHERS] + PLANE + COLUMN
    seen = []
    for delta in wanted:
        key = tuple(d % n for d, n in zip(delta, SIZES))
        if key not in seen:
            seen.append(key)
    return seen


def lanes(shape):
    return lax.broadcasted_iota(jnp.int32, shape, len(shape) - 1)


def sublanes(shape):
    return lax.broadcasted_iota(jnp.int32, shape, len(shape) - 2)


def row_sum(v):
    total = v[0:8]
    for k in range(8, v.shape[0], 8):
        total = total + v[k : k + 8]
    for shift in (4, 2, 1):
        total = total + pltpu.roll(total, shift, 0)
    return total


def main_kernel(
    orb_hbm, pot_hbm, atom_hbm, points_hbm, count_hbm, beta_hbm, coup_hbm,
    image_ref, gram_ref,
    psi, pot, pts, beta, coup, atom, count,
    zb, hy, pk, xb, msg, r1, a2, arow, sa, ba, sb, bb, rows16, onehot, spread,
    lsem, hsend, hrecv, csend, crecv,
):
    orb, ptsb = orb_hbm, points_hbm.at[0, 0, 0]
    loads = [
        pltpu.make_async_copy(orb, psi, lsem.at[0]),
        pltpu.make_async_copy(ptsb, pts, lsem.at[1]),
        pltpu.make_async_copy(beta_hbm.at[0, 0, 0], beta, lsem.at[2]),
        pltpu.make_async_copy(atom_hbm, atom, lsem.at[3]),
        pltpu.make_async_copy(count_hbm, count, lsem.at[4]),
        pltpu.make_async_copy(coup_hbm, coup, lsem.at[5]),
        pltpu.make_async_copy(pot_hbm, pot, lsem.at[6]),
    ]
    for load in loads:
        load.start()
    barrier = pltpu.get_barrier_semaphore()
    partners = all_partners()
    for delta in partners:
        pl.semaphore_signal(barrier, inc=1, device_id=at_offset(delta), device_id_type=MESH)

    def remote(src, dst, send, recv, delta):
        return pltpu.make_async_remote_copy(
            src_ref=src, dst_ref=dst, send_sem=send, recv_sem=recv,
            device_id=at_offset(delta), device_id_type=MESH,
        )

    def wait_bytes(ref, sem):
        pltpu.make_async_copy(ref, ref, sem).wait()

    lane8, sub8 = lanes((8, 128)), sublanes((8, 128))
    loads[0].wait()
    loads[1].wait()

    packed = jnp.zeros((8, 128), jnp.float32)
    for n in range(4):
        for z in range(4):
            g = n * 4 + z
            moved = pltpu.roll(psi[n, z], (4 + 8 * g) % 128, 1)
            packed = jnp.where(lane8 // 8 == g, moved, packed)
    pk[...] = packed

    lo = [pts[8 * h : 8 * h + 8] & 127 for h in range(2)]
    hi = [pts[8 * h : 8 * h + 8] >> 7 for h in range(2)]
    gathered = [[jnp.zeros((8, 128), jnp.float32) for _ in range(2)] for _ in range(4)]
    for row in range(32):
        pick = [hi[h] == row for h in range(2)]
        for n in range(4):
            line = jnp.broadcast_to(psi[n, row // 8, row % 8 : row % 8 + 1], (8, 128))
            for h in range(2):
                got = jnp.take_along_axis(line, lo[h], axis=1)
                gathered[n][h] = jnp.where(pick[h], got, gathered[n][h])

    for load in loads[2:]:
        load.wait()
    x, y, z = here()
    slots = count[0, 0, 0]
    dir_of, kind_of = [], []
    for b in range(16):
        a = atom[0, 0, 0, b]
        owner = a // 3
        dx = ((owner & 3) - x + 1) & 3
        dy = (((owner >> 2) & 7) - y + 1) & 7
        dz = ((owner >> 5) - z + 1) & 31
        where = jnp.minimum(jnp.maximum(dz * 9 + dy * 3 + dx, 0), 26)
        dir_of.append(where)
        kind_of.append(a - owner * 3)
    dir_lane = jnp.full((32, 128), 31, jnp.int32)
    for b in range(16):
        used = jnp.where(b < slots, dir_of[b], 31)
        dir_lane = jnp.where(lanes((32, 128)) // 8 == b, used, dir_lane)
    select = (sublanes((32, 128)) == dir_lane).astype(jnp.float32)

    lane_n, lane_k, lane_p = lane8 // 32, (lane8 // 8) & 3, lane8 & 7
    blocks = []
    for b in range(16):
        block = jnp.zeros((8, 128), jnp.float32)
        for n in range(4):
            line = jnp.broadcast_to(gathered[n][b // 8][b % 8 : b % 8 + 1], (8, 128))
            part = jnp.sum(beta[b] * line, axis=1, keepdims=True)
            block = jnp.where(lane_n == n, part, block)
        keep = (lane_p == sub8) & (lane_k == kind_of[b])
        blocks.append(jnp.where(keep, block, 0.0))
    msg[...] = jnp.dot(
        select, jnp.concatenate(blocks, axis=0), precision=HIGH, preferred_element_type=jnp.float32
    )

    pl.semaphore_wait(barrier, len(partners))
    for d in OTHERS:
        remote(msg.at[pl.ds(d, 1)], r1.at[pl.ds(d, 1)], csend.at[0], crecv.at[0], DIRS[d]).start()
    halo_copies = [
        (psi, zb.at[0]),
        (psi, zb.at[1]),
        (psi.at[:, :, pl.ds(4, 4)], hy.at[:, :, pl.ds(4, 4)]),
        (psi.at[:, :, pl.ds(0, 4)], hy.at[:, :, pl.ds(0, 4)]),
        (pk, xb.at[0]),
        (pk, xb.at[1]),
    ]
    halos = [
        remote(src, dst, hsend.at[k], hrecv.at[k], HALOS[k])
        for k, (src, dst) in reversed(list(enumerate(halo_copies)))
    ]
    for halo in halos:
        halo.start()
    r1[pl.ds(13, 1)] = msg[pl.ds(13, 1)]
    r1[pl.ds(27, 5)] = jnp.zeros((5, 128), jnp.float32)

    tiles = []
    for c in range(2):
        tile = jnp.concatenate([coup[c], jnp.zeros((8, 120), jnp.float32)], axis=1)
        for shift in (8, 16, 32, 64):
            tile = tile + pltpu.roll(tile, shift, 1)
        tiles.append(tile)
    couple = jnp.concatenate(
        [jnp.where(lane8 // 8 == r, tiles[0 if r % 4 == 0 else 1], 0.0) for r in range(16)], axis=0
    )
    li, si = lanes((128, 128)), sublanes((128, 128))
    away = (li - si) & 127
    away = jnp.minimum(away, 128 - away)
    along_x = jnp.where(away == 0, 3.0 * KIN[0], 0.0)
    for o in range(1, 5):
        along_x = jnp.where(away == o, KIN[o], along_x)
    sj, lj = si & 7, li & 7
    edge = jnp.zeros((128, 128), jnp.float32)
    for o in range(1, 5):
        left = (sj < 4) & (lj >= 4) & (lj - sj == o)
        right = (sj >= 4) & (lj < 4) & (sj - lj == o)
        edge = jnp.where((si // 8 == li // 8) & (left | right), KIN[o], edge)

    flat = psi[...].reshape(128, 128)
    base = jnp.dot(flat, along_x, precision=HIGH, preferred_element_type=jnp.float32)

    for b in range(16):
        line = jnp.broadcast_to(lo[b // 8][b % 8 : b % 8 + 1], (128, 128))
        onehot[:, pl.ds(b * 128, 128)] = (si == line).astype(jnp.bfloat16)

    for halo in halos:
        halo.wait_recv()
    change = jnp.where(lane8 & 7 < 4, xb[0], xb[1]) - pk[...]
    change = jnp.dot(change, edge, precision=HIGH, preferred_element_type=jnp.float32)
    at_edge = (lane8 < 4) | (lane8 >= 124)
    sums = [None] * len(PAIRS)
    for zz in range(4):
        image = []
        for n in range(4):
            own, other = psi[n, zz], hy[n, zz]
            total = base[(n * 4 + zz) * 8 : (n * 4 + zz) * 8 + 8]
            moved = pltpu.roll(change, (124 - 8 * (n * 4 + zz)) % 128, 1)
            total = total + jnp.where(at_edge, moved, 0.0)
            for o in range(1, 5):
                up = psi[n, zz + o] if zz + o < 4 else zb[1, n, zz + o - 4]
                down = psi[n, zz - o] if zz - o >= 0 else zb[0, n, zz - o + 4]
                before = pltpu.roll(jnp.where(sub8 < 8 - o, own, other), o, 0)
                after = pltpu.roll(jnp.where(sub8 >= o, own, other), 8 - o, 0)
                total = total + KIN[o] * ((up + down) + (before + after))
            total = total + pot[zz] * own
            image.append(total)
            image_ref[n, zz] = total
        for k, (i, j) in enumerate(PAIRS):
            term = psi[i, zz] * image[j]
            sums[k] = term if sums[k] is None else sums[k] + term
    local = jnp.zeros((8, 128), jnp.float32)
    for k, (i, j) in enumerate(PAIRS):
        total = jnp.sum(sums[k], axis=1, keepdims=True)
        local = jnp.where(lane8 == j * 32 + (j - i) * 8, total, local)

    wait_bytes(r1.at[pl.ds(0, 26)], crecv.at[0])
    coef = row_sum(r1[...])
    applied = jnp.dot(coef, couple, precision=HIGH, preferred_element_type=jnp.float32)
    arow[...] = applied
    turned = coef
    for s in range(1, 4):
        turned = jnp.where(sub8 == s, pltpu.roll(coef, 32 * s, 1), turned)
    outer = turned * applied
    outer = outer + (pltpu.roll(outer, 120, 1) + pltpu.roll(outer, 112, 1))
    outer = jnp.where((sub8 < 4) & (lane8 & 31 < 8), outer, 0.0)
    placed = local
    for s in range(4):
        placed = placed + jnp.where(sub8 == s, pltpu.roll(outer, 8 * s, 1) if s else outer, 0.0)
    placed = row_sum(placed)
    sa[...] = placed

    for k, delta in enumerate(PLANE):
        remote(sa.at[pl.ds(0, 1)], ba.at[pl.ds(k, 1)], csend.at[2], crecv.at[2], delta).start()
    for d in OTHERS:
        remote(arow.at[pl.ds(0, 1)], a2.at[pl.ds(26 - d, 1)], csend.at[1], crecv.at[1], DIRS[d]).start()
    a2[pl.ds(13, 1)] = arow[pl.ds(0, 1)]
    ba[pl.ds(31, 1)] = sa[pl.ds(0, 1)]
    wait_bytes(ba.at[pl.ds(0, 31)], crecv.at[2])
    sb[...] = row_sum(ba[...])
    for k, delta in enumerate(COLUMN):
        remote(sb.at[pl.ds(0, 1)], bb.at[pl.ds(k, 1)], csend.at[3], crecv.at[3], delta).start()
    bb[pl.ds(31, 1)] = sb[pl.ds(0, 1)]

    wait_bytes(a2.at[pl.ds(0, 26)], crecv.at[1])
    for b in range(16):
        rows16[pl.ds(b, 1)] = a2[pl.ds(dir_of[b], 1)]
    spots = []
    for h in range(2):
        kind = jnp.zeros((8, 128), jnp.int32)
        for b in range(8):
            kind = jnp.where(sub8 == b, kind_of[h * 8 + b], kind)
        spots.append(kind * 8 + lane_p)
    left = []
    for n in range(4):
        for h in range(2):
            got = jnp.take_along_axis(rows16[pl.ds(h * 8, 8)], spots[h] + 32 * n, axis=1)
            slot = sub8 + 8 * h
            left.append(jnp.where((lane8 // 8 == slot) & (slot < slots), got, 0.0))
    values = jnp.dot(
        jnp.concatenate(left, axis=0), beta[...].reshape(128, 128), precision=HIGH,
        preferred_element_type=jnp.float32,
    )
    high = values.astype(jnp.bfloat16).astype(jnp.float32)
    low = values - high
    for b in range(16):
        line = jnp.broadcast_to(hi[b // 8][b % 8 : b % 8 + 1], (32, 128))
        pick = sublanes((32, 128)) == line
        for part, source in enumerate((high, low)):
            for n in range(4):
                r = n * 16 + b
                piece = jnp.where(pick, jnp.broadcast_to(source[r : r + 1], (32, 128)), 0.0)
                spread[pl.ds(part * 128 + n * 32, 32), pl.ds(b * 128, 128)] = piece.astype(jnp.bfloat16)
    grid = lax.dot_general(
        spread[...], onehot[...], (((1,), (1,)), ((), ())), preferred_element_type=jnp.float32
    )
    projected = grid[0:128] + grid[128:256]
    image_ref[...] = image_ref[...] + projected.reshape(4, 4, 8, 128)

    wait_bytes(bb.at[pl.ds(0, 31)], crecv.at[3])
    gram_ref[...] = row_sum(bb[...])
    for halo in halos:
        halo.wait_send()
    wait_bytes(r1.at[pl.ds(0, 26)], csend.at[0])
    wait_bytes(a2.at[pl.ds(0, 26)], csend.at[1])
    wait_bytes(ba.at[pl.ds(0, 31)], csend.at[2])
    wait_bytes(bb.at[pl.ds(0, 31)], csend.at[3])


def residual_kernel(psi, image, gram, image_out, residual_out):
    lane8 = lanes((8, 128))
    row = gram[...]
    weight = {}
    for i, j in PAIRS:
        group = j * 4 + (j - i)
        total = jnp.sum(jnp.where(lane8 // 8 == group, row, 0.0), axis=1, keepdims=True)
        total = jnp.broadcast_to(total, (8, 128)) * (1.0 / GRID_TOTAL)
        weight[i, j] = weight[j, i] = total
    for z in range(4):
        for j in range(4):
            total = image[j, z]
            image_out[j, z] = total
            for i in range(4):
                total = total - weight[i, j] * psi[i, z]
            residual_out[j, z] = total


def on_device(orbitals, potential, block_atom, block_points, block_count, projector_values, coupling):
    f32, i32 = jnp.float32, jnp.int32
    anywhere = pl.BlockSpec(memory_space=pl.ANY)
    vmem = pl.BlockSpec(memory_space=pltpu.VMEM)
    field = jax.ShapeDtypeStruct((4, 4, 8, 128), f32)
    image, gram = pl.pallas_call(
        main_kernel,
        out_shape=(field, jax.ShapeDtypeStruct((8, 128), f32)),
        in_specs=[anywhere] * 7,
        out_specs=(vmem, vmem),
        scratch_shapes=[
            pltpu.VMEM((4, 4, 8, 128), f32),
            pltpu.VMEM((4, 8, 128), f32),
            pltpu.VMEM((16, 128), i32),
            pltpu.VMEM((16, 8, 128), f32),
            pltpu.VMEM((2, 8, 8), f32),
            pltpu.SMEM((1, 1, 1, 16), i32),
            pltpu.SMEM((1, 1, 1), i32),
            pltpu.VMEM((2, 4, 4, 8, 128), f32),
            pltpu.VMEM((4, 4, 8, 128), f32),
            pltpu.VMEM((8, 128), f32),
            pltpu.VMEM((2, 8, 128), f32),
            pltpu.VMEM((32, 128), f32),
            pltpu.VMEM((32, 128), f32),
            pltpu.VMEM((32, 128), f32),
            pltpu.VMEM((8, 128), f32),
            pltpu.VMEM((8, 128), f32),
            pltpu.VMEM((32, 128), f32),
            pltpu.VMEM((8, 128), f32),
            pltpu.VMEM((32, 128), f32),
            pltpu.VMEM((16, 128), f32),
            pltpu.VMEM((128, 2048), jnp.bfloat16),
            pltpu.VMEM((256, 2048), jnp.bfloat16),
            pltpu.SemaphoreType.DMA((7,)),
            pltpu.SemaphoreType.DMA((6,)),
            pltpu.SemaphoreType.DMA((6,)),
            pltpu.SemaphoreType.DMA((4,)),
            pltpu.SemaphoreType.DMA((4,)),
        ],
        compiler_params=pltpu.CompilerParams(
            collective_id=0, has_side_effects=True, vmem_limit_bytes=24 * 1024 * 1024
        ),
    )(orbitals, potential, block_atom, block_points, block_count, projector_values, coupling)
    return pl.pallas_call(
        residual_kernel,
        out_shape=(field, field),
        in_specs=[vmem] * 3,
        out_specs=(vmem, vmem),
    )(orbitals, image, gram)


def solution(mesh):
    return jax.shard_map(
        on_device,
        mesh=mesh,
        in_specs=(
            P(None, "gz", "gy", "gx"),
            P("gz", "gy", "gx"),
            P("gz", "gy", "gx", None),
            P("gz", "gy", "gx", None, None),
            P("gz", "gy", "gx"),
            P("gz", "gy", "gx", None, None, None),
            P(),
        ),
        out_specs=(P(None, "gz", "gy", "gx"), P(None, "gz", "gy", "gx")),
        check_vma=False,
    )
```

```python
import jax
import jax.numpy as jnp
from jax import lax
from jax.experimental import pallas as pl
from jax.experimental.pallas import tpu as pltpu
from jax.sharding import PartitionSpec as P

MESH = pl.DeviceIdType.MESH
HIGH = lax.Precision.HIGHEST
SIZES = (4, 8, 32)
GRID_TOTAL = 4194304
STENCIL = (-205.0 / 72.0, 8.0 / 5.0, -1.0 / 5.0, 8.0 / 315.0, -1.0 / 560.0)
KIN = tuple(-0.5 * c for c in STENCIL)
DIRS = [(d % 3 - 1, d // 3 % 3 - 1, d // 9 - 1) for d in range(27)]
OTHERS = [d for d in range(27) if d != 13]
PAIRS = [(i, j) for j in range(4) for i in range(j + 1)]
HALOS = [(0, 0, 1), (0, 0, -1), (0, 1, 0), (0, -1, 0), (1, 0, 0), (-1, 0, 0)]


def here():
    return lax.axis_index("gx"), lax.axis_index("gy"), lax.axis_index("gz")


def at_offset(delta):
    return tuple(
        v if d % n == 0 else (v + (d % n)) & (n - 1) for v, d, n in zip(here(), delta, SIZES)
    )


PLANE = [(0, 0, d) for d in range(1, 32)]
COLUMN = [(dx, dy, 0) for dx in range(4) for dy in range(8) if (dx, dy) != (0, 0)]


def all_partners():
    wanted = [DIRS[d] for d in OTHERS] + PLANE + COLUMN
    seen = []
    for delta in wanted:
        key = tuple(d % n for d, n in zip(delta, SIZES))
        if key not in seen:
            seen.append(key)
    return seen


def lanes(shape):
    return lax.broadcasted_iota(jnp.int32, shape, len(shape) - 1)


def sublanes(shape):
    return lax.broadcasted_iota(jnp.int32, shape, len(shape) - 2)


def row_sum(v):
    total = v[0:8]
    for k in range(8, v.shape[0], 8):
        total = total + v[k : k + 8]
    for shift in (4, 2, 1):
        total = total + pltpu.roll(total, shift, 0)
    return total


def main_kernel(
    orb_hbm, pot_hbm, atom_hbm, points_hbm, count_hbm, beta_hbm, coup_hbm,
    image_ref, gram_ref,
    psi, pot, pts, beta, coup, atom,
    zb, hy, pk, xb, msg, r1, a2, arow, sa, ba, sb, bb, rows16, onehot, spread,
    lsem, hsend, hrecv, csend, crecv,
):
    orb, ptsb = orb_hbm, points_hbm.at[0, 0, 0]
    loads = [
        pltpu.make_async_copy(orb, psi, lsem.at[0]),
        pltpu.make_async_copy(ptsb, pts, lsem.at[1]),
        pltpu.make_async_copy(beta_hbm.at[0, 0, 0], beta, lsem.at[2]),
        pltpu.make_async_copy(atom_hbm, atom, lsem.at[3]),
        pltpu.make_async_copy(coup_hbm, coup, lsem.at[5]),
        pltpu.make_async_copy(pot_hbm, pot, lsem.at[6]),
    ]
    for load in loads:
        load.start()
    barrier = pltpu.get_barrier_semaphore()
    partners = all_partners()
    for delta in partners:
        pl.semaphore_signal(barrier, inc=1, device_id=at_offset(delta), device_id_type=MESH)

    def remote(src, dst, send, recv, delta):
        return pltpu.make_async_remote_copy(
            src_ref=src, dst_ref=dst, send_sem=send, recv_sem=recv,
            device_id=at_offset(delta), device_id_type=MESH,
        )

    def wait_bytes(ref, sem):
        pltpu.make_async_copy(ref, ref, sem).wait()

    lane8, sub8 = lanes((8, 128)), sublanes((8, 128))
    loads[0].wait()
    loads[1].wait()

    packed = jnp.zeros((8, 128), jnp.float32)
    for n in range(4):
        for z in range(4):
            g = n * 4 + z
            moved = pltpu.roll(psi[n, z], (4 + 8 * g) % 128, 1)
            packed = jnp.where(lane8 // 8 == g, moved, packed)
    pk[...] = packed

    lo = [pts[8 * h : 8 * h + 8] & 127 for h in range(2)]
    hi = [pts[8 * h : 8 * h + 8] >> 7 for h in range(2)]
    gathered = [[jnp.zeros((8, 128), jnp.float32) for _ in range(2)] for _ in range(4)]
    for row in range(32):
        pick = [hi[h] == row for h in range(2)]
        for n in range(4):
            line = jnp.broadcast_to(psi[n, row // 8, row % 8 : row % 8 + 1], (8, 128))
            for h in range(2):
                got = jnp.take_along_axis(line, lo[h], axis=1)
                gathered[n][h] = jnp.where(pick[h], got, gathered[n][h])

    for load in loads[2:]:
        load.wait()
    x, y, z = here()
    slots = count_hbm[0, 0, 0]
    dir_of, kind_of = [], []
    for b in range(16):
        a = atom[0, 0, 0, b]
        owner = a // 3
        dx = ((owner & 3) - x + 1) & 3
        dy = (((owner >> 2) & 7) - y + 1) & 7
        dz = ((owner >> 5) - z + 1) & 31
        where = jnp.minimum(jnp.maximum(dz * 9 + dy * 3 + dx, 0), 26)
        dir_of.append(where)
        kind_of.append(a - owner * 3)
    dir_lane = jnp.full((32, 128), 31, jnp.int32)
    for b in range(16):
        used = jnp.where(b < slots, dir_of[b], 31)
        dir_lane = jnp.where(lanes((32, 128)) // 8 == b, used, dir_lane)
    select = (sublanes((32, 128)) == dir_lane).astype(jnp.float32)

    lane_n, lane_k, lane_p = lane8 // 32, (lane8 // 8) & 3, lane8 & 7
    blocks = []
    for b in range(16):
        block = jnp.zeros((8, 128), jnp.float32)
        for n in range(4):
            line = jnp.broadcast_to(gathered[n][b // 8][b % 8 : b % 8 + 1], (8, 128))
            part = jnp.sum(beta[b] * line, axis=1, keepdims=True)
            block = jnp.where(lane_n == n, part, block)
        keep = (lane_p == sub8) & (lane_k == kind_of[b])
        blocks.append(jnp.where(keep, block, 0.0))
    msg[...] = jnp.dot(
        select, jnp.concatenate(blocks, axis=0), precision=HIGH, preferred_element_type=jnp.float32
    )

    pl.semaphore_wait(barrier, len(partners))
    for d in OTHERS:
        remote(msg.at[pl.ds(d, 1)], r1.at[pl.ds(d, 1)], csend.at[0], crecv.at[0], DIRS[d]).start()
    halo_copies = [
        (psi, zb.at[0]),
        (psi, zb.at[1]),
        (psi.at[:, :, pl.ds(4, 4)], hy.at[:, :, pl.ds(4, 4)]),
        (psi.at[:, :, pl.ds(0, 4)], hy.at[:, :, pl.ds(0, 4)]),
        (pk, xb.at[0]),
        (pk, xb.at[1]),
    ]
    halos = [
        remote(src, dst, hsend.at[k], hrecv.at[k], HALOS[k])
        for k, (src, dst) in reversed(list(enumerate(halo_copies)))
    ]
    for halo in halos:
        halo.start()
    r1[pl.ds(13, 1)] = msg[pl.ds(13, 1)]
    r1[pl.ds(27, 5)] = jnp.zeros((5, 128), jnp.float32)

    tiles = []
    for c in range(2):
        tile = jnp.concatenate([coup[c], jnp.zeros((8, 120), jnp.float32)], axis=1)
        for shift in (8, 16, 32, 64):
            tile = tile + pltpu.roll(tile, shift, 1)
        tiles.append(tile)
    couple = jnp.concatenate(
        [jnp.where(lane8 // 8 == r, tiles[0 if r % 4 == 0 else 1], 0.0) for r in range(16)], axis=0
    )
    li, si = lanes((128, 128)), sublanes((128, 128))
    away = (li - si) & 127
    away = jnp.minimum(away, 128 - away)
    along_x = jnp.where(away == 0, 3.0 * KIN[0], 0.0)
    for o in range(1, 5):
        along_x = jnp.where(away == o, KIN[o], along_x)
    sj, lj = si & 7, li & 7
    edge = jnp.zeros((128, 128), jnp.float32)
    for o in range(1, 5):
        left = (sj < 4) & (lj >= 4) & (lj - sj == o)
        right = (sj >= 4) & (lj < 4) & (sj - lj == o)
        edge = jnp.where((si // 8 == li // 8) & (left | right), KIN[o], edge)

    flat = psi[...].reshape(128, 128)
    base = jnp.dot(flat, along_x, precision=HIGH, preferred_element_type=jnp.float32)

    for b in range(16):
        line = jnp.broadcast_to(lo[b // 8][b % 8 : b % 8 + 1], (128, 128))
        onehot[:, pl.ds(b * 128, 128)] = (si == line).astype(jnp.bfloat16)

    for halo in halos:
        halo.wait_recv()
    change = jnp.where(lane8 & 7 < 4, xb[0], xb[1]) - pk[...]
    change = jnp.dot(change, edge, precision=HIGH, preferred_element_type=jnp.float32)
    at_edge = (lane8 < 4) | (lane8 >= 124)
    sums = [None] * len(PAIRS)
    for zz in range(4):
        image = []
        for n in range(4):
            own, other = psi[n, zz], hy[n, zz]
            total = base[(n * 4 + zz) * 8 : (n * 4 + zz) * 8 + 8]
            moved = pltpu.roll(change, (124 - 8 * (n * 4 + zz)) % 128, 1)
            total = total + jnp.where(at_edge, moved, 0.0)
            for o in range(1, 5):
                up = psi[n, zz + o] if zz + o < 4 else zb[1, n, zz + o - 4]
                down = psi[n, zz - o] if zz - o >= 0 else zb[0, n, zz - o + 4]
                before = pltpu.roll(jnp.where(sub8 < 8 - o, own, other), o, 0)
                after = pltpu.roll(jnp.where(sub8 >= o, own, other), 8 - o, 0)
                total = total + KIN[o] * ((up + down) + (before + after))
            total = total + pot[zz] * own
            image.append(total)
            image_ref[n, zz] = total
        for k, (i, j) in enumerate(PAIRS):
            term = psi[i, zz] * image[j]
            sums[k] = term if sums[k] is None else sums[k] + term
    local = jnp.zeros((8, 128), jnp.float32)
    for k, (i, j) in enumerate(PAIRS):
        total = jnp.sum(sums[k], axis=1, keepdims=True)
        local = jnp.where(lane8 == j * 32 + (j - i) * 8, total, local)

    wait_bytes(r1.at[pl.ds(0, 26)], crecv.at[0])
    coef = row_sum(r1[...])
    applied = jnp.dot(coef, couple, precision=HIGH, preferred_element_type=jnp.float32)
    arow[...] = applied
    turned = coef
    for s in range(1, 4):
        turned = jnp.where(sub8 == s, pltpu.roll(coef, 32 * s, 1), turned)
    outer = turned * applied
    outer = outer + (pltpu.roll(outer, 120, 1) + pltpu.roll(outer, 112, 1))
    outer = jnp.where((sub8 < 4) & (lane8 & 31 < 8), outer, 0.0)
    placed = local
    for s in range(4):
        placed = placed + jnp.where(sub8 == s, pltpu.roll(outer, 8 * s, 1) if s else outer, 0.0)
    placed = row_sum(placed)
    sa[...] = placed

    for k, delta in enumerate(PLANE):
        remote(sa.at[pl.ds(0, 1)], ba.at[pl.ds(k, 1)], csend.at[2], crecv.at[2], delta).start()
    for d in OTHERS:
        remote(arow.at[pl.ds(0, 1)], a2.at[pl.ds(26 - d, 1)], csend.at[1], crecv.at[1], DIRS[d]).start()
    a2[pl.ds(13, 1)] = arow[pl.ds(0, 1)]
    ba[pl.ds(31, 1)] = sa[pl.ds(0, 1)]
    wait_bytes(ba.at[pl.ds(0, 31)], crecv.at[2])
    sb[...] = row_sum(ba[...])
    for k, delta in enumerate(COLUMN):
        remote(sb.at[pl.ds(0, 1)], bb.at[pl.ds(k, 1)], csend.at[3], crecv.at[3], delta).start()
    bb[pl.ds(31, 1)] = sb[pl.ds(0, 1)]

    wait_bytes(a2.at[pl.ds(0, 26)], crecv.at[1])
    for b in range(16):
        rows16[pl.ds(b, 1)] = a2[pl.ds(dir_of[b], 1)]
    spots = []
    for h in range(2):
        kind = jnp.zeros((8, 128), jnp.int32)
        for b in range(8):
            kind = jnp.where(sub8 == b, kind_of[h * 8 + b], kind)
        spots.append(kind * 8 + lane_p)
    left = []
    for n in range(4):
        for h in range(2):
            got = jnp.take_along_axis(rows16[pl.ds(h * 8, 8)], spots[h] + 32 * n, axis=1)
            slot = sub8 + 8 * h
            left.append(jnp.where((lane8 // 8 == slot) & (slot < slots), got, 0.0))
    values = jnp.dot(
        jnp.concatenate(left, axis=0), beta[...].reshape(128, 128), precision=HIGH,
        preferred_element_type=jnp.float32,
    )
    high = values.astype(jnp.bfloat16).astype(jnp.float32)
    low = values - high
    for b in range(16):
        line = jnp.broadcast_to(hi[b // 8][b % 8 : b % 8 + 1], (32, 128))
        pick = sublanes((32, 128)) == line
        for part, source in enumerate((high, low)):
            for n in range(4):
                r = n * 16 + b
                piece = jnp.where(pick, jnp.broadcast_to(source[r : r + 1], (32, 128)), 0.0)
                spread[pl.ds(part * 128 + n * 32, 32), pl.ds(b * 128, 128)] = piece.astype(jnp.bfloat16)
    grid = lax.dot_general(
        spread[...], onehot[...], (((1,), (1,)), ((), ())), preferred_element_type=jnp.float32
    )
    projected = grid[0:128] + grid[128:256]
    image_ref[...] = image_ref[...] + projected.reshape(4, 4, 8, 128)

    wait_bytes(bb.at[pl.ds(0, 31)], crecv.at[3])
    gram_ref[...] = row_sum(bb[...])
    for halo in halos:
        halo.wait_send()
    wait_bytes(r1.at[pl.ds(0, 26)], csend.at[0])
    wait_bytes(a2.at[pl.ds(0, 26)], csend.at[1])
    wait_bytes(ba.at[pl.ds(0, 31)], csend.at[2])
    wait_bytes(bb.at[pl.ds(0, 31)], csend.at[3])


def residual_kernel(psi, image, gram, image_out, residual_out, residual, sem):
    copies = [pltpu.make_async_copy(image, image_out, sem.at[4])]
    copies[0].start()
    lane8 = lanes((8, 128))
    row = gram[...]
    weight = {}
    for i, j in PAIRS:
        group = j * 4 + (j - i)
        total = jnp.sum(jnp.where(lane8 // 8 == group, row, 0.0), axis=1, keepdims=True)
        total = jnp.broadcast_to(total, (8, 128)) * (1.0 / GRID_TOTAL)
        weight[i, j] = weight[j, i] = total
    for j in range(4):
        for z in range(4):
            total = image[j, z]
            for i in range(4):
                total = total - weight[i, j] * psi[i, z]
            residual[j, z] = total
        copies.append(pltpu.make_async_copy(residual.at[j], residual_out.at[j], sem.at[j]))
        copies[-1].start()
    for copy in copies:
        copy.wait()


def on_device(orbitals, potential, block_atom, block_points, block_count, projector_values, coupling):
    f32, i32 = jnp.float32, jnp.int32
    hbm = pl.BlockSpec(memory_space=pl.ANY)
    vmem = pl.BlockSpec(memory_space=pltpu.VMEM)
    field = jax.ShapeDtypeStruct((4, 4, 8, 128), f32)
    held = [
        pltpu.with_memory_space_constraint(v, pltpu.HBM)
        for v in (orbitals, potential, block_atom, block_points, projector_values, coupling)
    ]
    held.insert(4, block_count)
    image, gram = pl.pallas_call(
        main_kernel,
        out_shape=(pltpu.VMEM((4, 4, 8, 128), f32), pltpu.VMEM((8, 128), f32)),
        in_specs=[hbm] * 4 + [pl.BlockSpec(memory_space=pltpu.SMEM)] + [hbm] * 2,
        out_specs=(vmem, vmem),
        scratch_shapes=[
            pltpu.VMEM((4, 4, 8, 128), f32),
            pltpu.VMEM((4, 8, 128), f32),
            pltpu.VMEM((16, 128), i32),
            pltpu.VMEM((16, 8, 128), f32),
            pltpu.VMEM((2, 8, 8), f32),
            pltpu.SMEM((1, 1, 1, 16), i32),
            pltpu.VMEM((2, 4, 4, 8, 128), f32),
            pltpu.VMEM((4, 4, 8, 128), f32),
            pltpu.VMEM((8, 128), f32),
            pltpu.VMEM((2, 8, 128), f32),
            pltpu.VMEM((32, 128), f32),
            pltpu.VMEM((32, 128), f32),
            pltpu.VMEM((32, 128), f32),
            pltpu.VMEM((8, 128), f32),
            pltpu.VMEM((8, 128), f32),
            pltpu.VMEM((32, 128), f32),
            pltpu.VMEM((8, 128), f32),
            pltpu.VMEM((32, 128), f32),
            pltpu.VMEM((16, 128), f32),
            pltpu.VMEM((128, 2048), jnp.bfloat16),
            pltpu.VMEM((256, 2048), jnp.bfloat16),
            pltpu.SemaphoreType.DMA((7,)),
            pltpu.SemaphoreType.DMA((6,)),
            pltpu.SemaphoreType.DMA((6,)),
            pltpu.SemaphoreType.DMA((4,)),
            pltpu.SemaphoreType.DMA((4,)),
        ],
        compiler_params=pltpu.CompilerParams(
            collective_id=0, has_side_effects=True, vmem_limit_bytes=24 * 1024 * 1024
        ),
    )(*held)
    return pl.pallas_call(
        residual_kernel,
        out_shape=(field, field),
        in_specs=[vmem] * 3,
        out_specs=(hbm, hbm),
        scratch_shapes=[pltpu.VMEM((4, 4, 8, 128), f32), pltpu.SemaphoreType.DMA((5,))],
        compiler_params=pltpu.CompilerParams(vmem_limit_bytes=16 * 1024 * 1024),
    )(orbitals, image, gram)


def solution(mesh):
    return jax.shard_map(
        on_device,
        mesh=mesh,
        in_specs=(
            P(None, "gz", "gy", "gx"),
            P("gz", "gy", "gx"),
            P("gz", "gy", "gx", None),
            P("gz", "gy", "gx", None, None),
            P("gz", "gy", "gx"),
            P("gz", "gy", "gx", None, None, None),
            P(),
        ),
        out_specs=(P(None, "gz", "gy", "gx"), P(None, "gz", "gy", "gx")),
        check_vma=False,
    )
```

```python
import jax
import jax.numpy as jnp
from jax import lax
from jax.experimental import pallas as pl
from jax.experimental.pallas import tpu as pltpu
from jax.sharding import PartitionSpec as P

MESH = pl.DeviceIdType.MESH
HIGH = lax.Precision.HIGHEST
SIZES = (4, 8, 32)
GRID_TOTAL = 4194304
STENCIL = (-205.0 / 72.0, 8.0 / 5.0, -1.0 / 5.0, 8.0 / 315.0, -1.0 / 560.0)
KIN = tuple(-0.5 * c for c in STENCIL)
PAIRS = [(i, j) for j in range(4) for i in range(j + 1)]
HALOS = [(0, 0, 1), (0, 0, -1), (0, 1, 0), (0, -1, 0)]
PLANE = [(0, 0, d) for d in range(1, 32)]
SIDES = (-1, 0, 1)


def here():
    return lax.axis_index("gx"), lax.axis_index("gy"), lax.axis_index("gz")


def at_offset(delta):
    return tuple(
        v if d % n == 0 else (v + (d % n)) & (n - 1) for v, d, n in zip(here(), delta, SIZES)
    )


def lanes(shape):
    return lax.broadcasted_iota(jnp.int32, shape, len(shape) - 1)


def sublanes(shape):
    return lax.broadcasted_iota(jnp.int32, shape, len(shape) - 2)


def row_sum(v):
    total = v[0:8]
    for k in range(8, v.shape[0], 8):
        total = total + v[k : k + 8]
    for shift in (4, 2, 1):
        total = total + pltpu.roll(total, shift, 0)
    return total


def main_kernel(
    orb_hbm, pot_hbm, atom_hbm, points_hbm, count, beta_hbm, coup_hbm,
    image_ref, gram_ref,
    psi, pot, pts, beta, coup, atom,
    zb, hy, pk, xcor, msg, a2, row_own, rows16, onehot, spread,
    r1, pe, xc, kr, stage, row_hub, ba, row_all, xrow,
    lsem, hsend, hrecv, csend, crecv,
):
    f32 = jnp.float32
    loads = [
        pltpu.make_async_copy(orb_hbm, psi, lsem.at[0]),
        pltpu.make_async_copy(points_hbm.at[0, 0, 0], pts, lsem.at[1]),
        pltpu.make_async_copy(beta_hbm.at[0, 0, 0], beta, lsem.at[2]),
        pltpu.make_async_copy(atom_hbm, atom, lsem.at[3]),
        pltpu.make_async_copy(coup_hbm, coup, lsem.at[4]),
        pltpu.make_async_copy(pot_hbm, pot, lsem.at[5]),
    ]
    for load in loads:
        load.start()
    x, y, z = here()
    column = x * 8 + y
    is_hub = column == 0

    def hub_of(d):
        return (0, 0, (z + d) & 31)

    def member(c, d):
        return (c >> 3, c & 7, (z + d) & 31)

    barrier = pltpu.get_barrier_semaphore()

    def greet(device):
        pl.semaphore_signal(barrier, inc=1, device_id=device, device_id_type=MESH)

    for delta in reversed(HALOS):
        greet(at_offset(delta))
    for d in (-1, 1):
        greet(hub_of(d))

    @pl.when(jnp.logical_not(is_hub))
    def _():
        greet(hub_of(0))

    @pl.when(is_hub)
    def _():
        for d in (-1, 1):
            greet(hub_of(d))

        def each(c, carry):
            for d in SIDES:
                greet(member(c, d))
            greet(hub_of(c))
            return carry

        lax.fori_loop(1, 32, each, 0)

    def remote(src, dst, send, recv, device):
        return pltpu.make_async_remote_copy(
            src_ref=src, dst_ref=dst, send_sem=send, recv_sem=recv,
            device_id=device, device_id_type=MESH,
        )

    def wait_bytes(ref, sem):
        pltpu.make_async_copy(ref, ref, sem).wait()

    lane8, sub8 = lanes((8, 128)), sublanes((8, 128))
    loads[0].wait()

    packed = jnp.zeros((8, 128), f32)
    for n in range(4):
        for zz in range(4):
            g = n * 4 + zz
            moved = pltpu.roll(psi[n, zz], (4 + 8 * g) % 128, 1)
            packed = jnp.where(lane8 // 8 == g, moved, packed)
    pk[...] = packed

    pl.semaphore_wait(barrier, jnp.where(is_hub, 4 + 2 + 2 + 31 * 4, 4 + 3))
    halo_copies = [
        (psi, zb.at[0]),
        (psi, zb.at[1]),
        (psi.at[:, :, pl.ds(4, 4)], hy.at[:, :, pl.ds(4, 4)]),
        (psi.at[:, :, pl.ds(0, 4)], hy.at[:, :, pl.ds(0, 4)]),
    ]
    halos = [
        remote(src, dst, hsend.at[k], hrecv.at[k], at_offset(HALOS[k]))
        for k, (src, dst) in enumerate(halo_copies)
    ]
    for halo in halos:
        halo.start()

    @pl.when(jnp.logical_not(is_hub))
    def _():
        remote(pk, pe.at[column], csend.at[4], crecv.at[4], hub_of(0)).start()

    loads[1].wait()
    lo = [pts[8 * h : 8 * h + 8] & 127 for h in range(2)]
    hi = [pts[8 * h : 8 * h + 8] >> 7 for h in range(2)]
    gathered = [[jnp.zeros((8, 128), f32) for _ in range(2)] for _ in range(4)]
    for row in range(32):
        pick = [hi[h] == row for h in range(2)]
        for n in range(4):
            line = jnp.broadcast_to(psi[n, row // 8, row % 8 : row % 8 + 1], (8, 128))
            for h in range(2):
                got = jnp.take_along_axis(line, lo[h], axis=1)
                gathered[n][h] = jnp.where(pick[h], got, gathered[n][h])

    for load in loads[2:]:
        load.wait()
    slots = count[0, 0, 0]
    dir_of, kind_of = [], []
    for b in range(16):
        a = atom[0, 0, 0, b]
        owner = a // 3
        dx = ((owner & 3) - x + 1) & 3
        dy = (((owner >> 2) & 7) - y + 1) & 7
        dz = ((owner >> 5) - z + 1) & 31
        where = jnp.minimum(jnp.maximum(dz * 16 + dy * 3 + dx, 0), 47)
        dir_of.append(where)
        kind_of.append(a - owner * 3)
    dir_lane = jnp.full((48, 128), 63, jnp.int32)
    for b in range(16):
        used = jnp.where(b < slots, dir_of[b], 63)
        dir_lane = jnp.where(lanes((48, 128)) // 8 == b, used, dir_lane)
    select = (sublanes((48, 128)) == dir_lane).astype(f32)

    lane_n, lane_k, lane_p = lane8 // 32, (lane8 // 8) & 3, lane8 & 7
    blocks = []
    for b in range(16):
        block = jnp.zeros((8, 128), f32)
        for n in range(4):
            line = jnp.broadcast_to(gathered[n][b // 8][b % 8 : b % 8 + 1], (8, 128))
            part = jnp.sum(beta[b] * line, axis=1, keepdims=True)
            block = jnp.where(lane_n == n, part, block)
        keep = (lane_p == sub8) & (lane_k == kind_of[b])
        blocks.append(jnp.where(keep, block, 0.0))
    msg[...] = jnp.dot(
        select, jnp.concatenate(blocks, axis=0), precision=HIGH, preferred_element_type=f32
    )

    def send_rows(d):
        src, dst = msg.at[pl.ds(16 * (d + 1), 9)], r1.at[32 * (d + 1) + column, pl.ds(0, 9)]
        remote(src, dst, csend.at[0], crecv.at[0], hub_of(d)).start()

    send_rows(-1)
    send_rows(1)

    @pl.when(jnp.logical_not(is_hub))
    def _():
        send_rows(0)

    li, si = lanes((128, 128)), sublanes((128, 128))
    away = (li - si) & 127
    away = jnp.minimum(away, 128 - away)
    along_x = jnp.where(away == 0, 3.0 * KIN[0], 0.0)
    for o in range(1, 5):
        along_x = jnp.where(away == o, KIN[o], along_x)
    flat = psi[...].reshape(128, 128)
    base = jnp.dot(flat, along_x, precision=HIGH, preferred_element_type=f32)

    for b in range(16):
        line = jnp.broadcast_to(lo[b // 8][b % 8 : b % 8 + 1], (128, 128))
        onehot[:, pl.ds(b * 128, 128)] = (si == line).astype(jnp.bfloat16)

    for halo in halos:
        halo.wait_recv()
    sums = [None] * len(PAIRS)
    for zz in range(4):
        image = []
        for n in range(4):
            own, other = psi[n, zz], hy[n, zz]
            total = base[(n * 4 + zz) * 8 : (n * 4 + zz) * 8 + 8]
            for o in range(1, 5):
                up = psi[n, zz + o] if zz + o < 4 else zb[1, n, zz + o - 4]
                down = psi[n, zz - o] if zz - o >= 0 else zb[0, n, zz - o + 4]
                before = pltpu.roll(jnp.where(sub8 < 8 - o, own, other), o, 0)
                after = pltpu.roll(jnp.where(sub8 >= o, own, other), 8 - o, 0)
                total = total + KIN[o] * ((up + down) + (before + after))
            total = total + pot[zz] * own
            image.append(total)
            image_ref[n, zz] = total
        for k, (i, j) in enumerate(PAIRS):
            term = psi[i, zz] * image[j]
            sums[k] = term if sums[k] is None else sums[k] + term
    local = jnp.zeros((8, 128), f32)
    for k, (i, j) in enumerate(PAIRS):
        total = jnp.sum(sums[k], axis=1, keepdims=True)
        local = jnp.where(lane8 == j * 32 + (j - i) * 8, total, local)
    row_own[...] = row_sum(local)

    @pl.when(jnp.logical_not(is_hub))
    def _():
        remote(
            row_own.at[pl.ds(0, 1)], kr.at[column, pl.ds(0, 1)], csend.at[5], crecv.at[5], hub_of(0)
        ).start()

    @pl.when(is_hub)
    def _():
        kr[0] = row_own[...]
        pe[0] = pk[...]
        r1[32, pl.ds(0, 9)] = msg[pl.ds(16, 9)]
        sj, lj = si & 7, li & 7
        edge = jnp.zeros((128, 128), f32)
        for o in range(1, 5):
            left = (sj < 4) & (lj >= 4) & (lj - sj == o)
            right = (sj >= 4) & (lj < 4) & (sj - lj == o)
            edge = jnp.where((si // 8 == li // 8) & (left | right), KIN[o], edge)
        tiles = []
        for c in range(2):
            tile = jnp.concatenate([coup[c], jnp.zeros((8, 120), f32)], axis=1)
            for shift in (8, 16, 32, 64):
                tile = tile + pltpu.roll(tile, shift, 1)
            tiles.append(tile)
        couple = jnp.concatenate(
            [jnp.where(lane8 // 8 == r, tiles[0 if r % 4 == 0 else 1], 0.0) for r in range(16)],
            axis=0,
        )

        def reaches(box, c, r):
            third = (r * 11) >> 5
            tx = ((c >> 3) + (r - 3 * third) + 3) & 3
            ty = ((c & 7) + third + 7) & 7
            return ((r < 9) & (box == tx * 8 + ty)).astype(f32)

        col, box = lanes((32, 512)), sublanes((32, 512))
        collect = reaches(box, col >> 4, col & 15)
        row, box = sublanes((512, 32)), lanes((512, 32))
        spread_out = reaches(box, row >> 4, row & 15)

        wait_bytes(pe.at[pl.ds(0, 31)], crecv.at[4])
        edges = []
        for c in range(32):
            before, after = (c + 24) % 32, (c + 8) % 32
            edges.append(jnp.where(lane8 & 7 < 4, pe[before], pe[after]) - pe[c])
        change = jnp.dot(
            jnp.concatenate(edges, axis=0), edge, precision=HIGH, preferred_element_type=f32
        )
        outer = [jnp.zeros((8, 128), f32) for _ in range(4)]
        for c in range(32):
            part = change[8 * c : 8 * c + 8]
            xc[c] = part
            for s in range(4):
                outer[s] = outer[s] + (pltpu.roll(pe[c], 32 * s, 1) if s else pe[c]) * part

        wait_bytes(r1.at[pl.ds(0, 95), pl.ds(0, 9)], crecv.at[0])
        gathered_rows = (r1[pl.ds(0, 32)] + r1[pl.ds(64, 32)]) + r1[pl.ds(32, 32)]
        gathered_rows = jnp.where(sublanes((32, 16, 128)) < 9, gathered_rows, 0.0)
        coef = jnp.dot(
            collect, gathered_rows.reshape(512, 128), precision=HIGH, preferred_element_type=f32
        )
        applied = jnp.dot(coef, couple, precision=HIGH, preferred_element_type=f32)
        stage[...] = jnp.dot(
            spread_out, applied, precision=HIGH, preferred_element_type=f32
        ).reshape(32, 16, 128)

        def hand_out(c, d):
            remote(
                stage.at[c, pl.ds(0, 9)], a2.at[pl.ds(16 * (1 - d), 9)], csend.at[1], crecv.at[1],
                member(c, d),
            ).start()

        def each(c, carry):
            for d in SIDES:
                hand_out(c, d)
            remote(xc.at[c], xcor, csend.at[6], crecv.at[6], member(c, 0)).start()
            return carry

        hand_out(0, -1)
        hand_out(0, 1)
        lax.fori_loop(1, 32, each, 0)
        a2[pl.ds(16, 9)] = stage[0, pl.ds(0, 9)]
        xcor[...] = xc[0]

        for v in range(4):
            c8, a8 = coef[8 * v : 8 * v + 8], applied[8 * v : 8 * v + 8]
            for s in range(4):
                outer[s] = outer[s] + (pltpu.roll(c8, 32 * s, 1) if s else c8) * a8
        placed = jnp.zeros((8, 128), f32)
        for s in range(4):
            part = outer[s]
            part = (part + pltpu.roll(part, 120, 1)) + (pltpu.roll(part, 112, 1) + pltpu.roll(part, 104, 1))
            part = jnp.where(lane8 & 31 < 8, part, 0.0)
            placed = placed + (pltpu.roll(part, 8 * s, 1) if s else part)
        placed = row_sum(placed)
        wait_bytes(kr.at[pl.ds(0, 31), pl.ds(0, 1)], crecv.at[5])
        kinetic = kr[0]
        for c in range(1, 32):
            kinetic = kinetic + kr[c]
        row_hub[...] = placed + kinetic
        ba[pl.ds(31, 1)] = row_hub[pl.ds(0, 1)]
        for k, delta in enumerate(PLANE):
            remote(
                row_hub.at[pl.ds(0, 1)], ba.at[pl.ds(k, 1)], csend.at[2], crecv.at[2], at_offset(delta)
            ).start()

    @pl.when(is_hub)
    def _():
        wait_bytes(a2.at[pl.ds(0, 18)], crecv.at[1])

    @pl.when(jnp.logical_not(is_hub))
    def _():
        wait_bytes(a2.at[pl.ds(0, 27)], crecv.at[1])
        wait_bytes(xcor, crecv.at[6])

    for b in range(16):
        rows16[pl.ds(b, 1)] = a2[pl.ds(dir_of[b], 1)]
    spots = []
    for h in range(2):
        kind = jnp.zeros((8, 128), jnp.int32)
        for b in range(8):
            kind = jnp.where(sub8 == b, kind_of[h * 8 + b], kind)
        spots.append(kind * 8 + lane_p)
    left = []
    for n in range(4):
        for h in range(2):
            got = jnp.take_along_axis(rows16[pl.ds(h * 8, 8)], spots[h] + 32 * n, axis=1)
            slot = sub8 + 8 * h
            left.append(jnp.where((lane8 // 8 == slot) & (slot < slots), got, 0.0))
    values = jnp.dot(
        jnp.concatenate(left, axis=0), beta[...].reshape(128, 128), precision=HIGH,
        preferred_element_type=f32,
    )
    high = values.astype(jnp.bfloat16).astype(f32)
    low = values - high
    for b in range(16):
        line = jnp.broadcast_to(hi[b // 8][b % 8 : b % 8 + 1], (32, 128))
        pick = sublanes((32, 128)) == line
        for part, source in enumerate((high, low)):
            for n in range(4):
                r = n * 16 + b
                piece = jnp.where(pick, jnp.broadcast_to(source[r : r + 1], (32, 128)), 0.0)
                spread[pl.ds(part * 128 + n * 32, 32), pl.ds(b * 128, 128)] = piece.astype(jnp.bfloat16)
    grid = lax.dot_general(
        spread[...], onehot[...], (((1,), (1,)), ((), ())), preferred_element_type=f32
    )
    at_edge = (lane8 < 4) | (lane8 >= 124)
    for n in range(4):
        for zz in range(4):
            g = n * 4 + zz
            moved = pltpu.roll(xcor[...], (124 - 8 * g) % 128, 1)
            projected = grid[8 * g : 8 * g + 8] + grid[128 + 8 * g : 136 + 8 * g]
            image_ref[n, zz] = image_ref[n, zz] + jnp.where(at_edge, moved, 0.0) + projected

    @pl.when(is_hub)
    def _():
        wait_bytes(ba.at[pl.ds(0, 31)], crecv.at[2])
        row_all[...] = row_sum(ba[...])

        def each(c, carry):
            row = row_all.at[pl.ds(0, 1)]
            remote(row, xrow.at[pl.ds(0, 1)], csend.at[3], crecv.at[3], member(c, 0)).start()
            return carry

        lax.fori_loop(1, 32, each, 0)
        gram_ref[...] = row_all[...]
        wait_bytes(msg.at[pl.ds(0, 18)], csend.at[0])
        wait_bytes(r1.at[pl.ds(0, 95), pl.ds(0, 9)], csend.at[1])
        wait_bytes(pe.at[pl.ds(0, 31)], csend.at[6])
        wait_bytes(ba.at[pl.ds(0, 31)], csend.at[2])
        wait_bytes(kr.at[pl.ds(0, 31), pl.ds(0, 1)], csend.at[3])

    @pl.when(jnp.logical_not(is_hub))
    def _():
        wait_bytes(xrow.at[pl.ds(0, 1)], crecv.at[3])
        gram_ref[...] = jnp.broadcast_to(xrow[pl.ds(0, 1)], (8, 128))
        wait_bytes(msg.at[pl.ds(0, 27)], csend.at[0])
        wait_bytes(pk, csend.at[4])
        wait_bytes(row_own.at[pl.ds(0, 1)], csend.at[5])

    for halo in halos:
        halo.wait_send()


def residual_kernel(psi, image, gram, image_out, residual_out, residual, sem):
    copies = [pltpu.make_async_copy(image, image_out, sem.at[4])]
    copies[0].start()
    lane8 = lanes((8, 128))
    row = gram[...]
    weight = {}
    for i, j in PAIRS:
        group = j * 4 + (j - i)
        total = jnp.sum(jnp.where(lane8 // 8 == group, row, 0.0), axis=1, keepdims=True)
        total = jnp.broadcast_to(total, (8, 128)) * (1.0 / GRID_TOTAL)
        weight[i, j] = weight[j, i] = total
    for j in range(4):
        for z in range(4):
            total = image[j, z]
            for i in range(4):
                total = total - weight[i, j] * psi[i, z]
            residual[j, z] = total
        copies.append(pltpu.make_async_copy(residual.at[j], residual_out.at[j], sem.at[j]))
        copies[-1].start()
    for copy in copies:
        copy.wait()


def on_device(orbitals, potential, block_atom, block_points, block_count, projector_values, coupling):
    f32, i32 = jnp.float32, jnp.int32
    hbm = pl.BlockSpec(memory_space=pl.ANY)
    vmem = pl.BlockSpec(memory_space=pltpu.VMEM)
    field = jax.ShapeDtypeStruct((4, 4, 8, 128), f32)
    held = [
        pltpu.with_memory_space_constraint(v, pltpu.HBM)
        for v in (orbitals, potential, block_atom, block_points, projector_values, coupling)
    ]
    held.insert(4, block_count)
    image, gram = pl.pallas_call(
        main_kernel,
        out_shape=(pltpu.VMEM((4, 4, 8, 128), f32), pltpu.VMEM((8, 128), f32)),
        in_specs=[hbm] * 4 + [pl.BlockSpec(memory_space=pltpu.SMEM)] + [hbm] * 2,
        out_specs=(vmem, vmem),
        scratch_shapes=[
            pltpu.VMEM((4, 4, 8, 128), f32),
            pltpu.VMEM((4, 8, 128), f32),
            pltpu.VMEM((16, 128), i32),
            pltpu.VMEM((16, 8, 128), f32),
            pltpu.VMEM((2, 8, 8), f32),
            pltpu.SMEM((1, 1, 1, 16), i32),
            pltpu.VMEM((2, 4, 4, 8, 128), f32),
            pltpu.VMEM((4, 4, 8, 128), f32),
            pltpu.VMEM((8, 128), f32),
            pltpu.VMEM((8, 128), f32),
            pltpu.VMEM((48, 128), f32),
            pltpu.VMEM((48, 128), f32),
            pltpu.VMEM((8, 128), f32),
            pltpu.VMEM((16, 128), f32),
            pltpu.VMEM((128, 2048), jnp.bfloat16),
            pltpu.VMEM((256, 2048), jnp.bfloat16),
            pltpu.VMEM((96, 16, 128), f32),
            pltpu.VMEM((32, 8, 128), f32),
            pltpu.VMEM((32, 8, 128), f32),
            pltpu.VMEM((32, 8, 128), f32),
            pltpu.VMEM((32, 16, 128), f32),
            pltpu.VMEM((8, 128), f32),
            pltpu.VMEM((32, 128), f32),
            pltpu.VMEM((8, 128), f32),
            pltpu.VMEM((8, 128), f32),
            pltpu.SemaphoreType.DMA((6,)),
            pltpu.SemaphoreType.DMA((4,)),
            pltpu.SemaphoreType.DMA((4,)),
            pltpu.SemaphoreType.DMA((7,)),
            pltpu.SemaphoreType.DMA((7,)),
        ],
        compiler_params=pltpu.CompilerParams(
            collective_id=0, has_side_effects=True, vmem_limit_bytes=24 * 1024 * 1024
        ),
    )(*held)
    return pl.pallas_call(
        residual_kernel,
        out_shape=(field, field),
        in_specs=[vmem] * 3,
        out_specs=(hbm, hbm),
        scratch_shapes=[pltpu.VMEM((4, 4, 8, 128), f32), pltpu.SemaphoreType.DMA((5,))],
        compiler_params=pltpu.CompilerParams(vmem_limit_bytes=16 * 1024 * 1024),
    )(orbitals, image, gram)


def solution(mesh):
    return jax.shard_map(
        on_device,
        mesh=mesh,
        in_specs=(
            P(None, "gz", "gy", "gx"),
            P("gz", "gy", "gx"),
            P("gz", "gy", "gx", None),
            P("gz", "gy", "gx", None, None),
            P("gz", "gy", "gx"),
            P("gz", "gy", "gx", None, None, None),
            P(),
        ),
        out_specs=(P(None, "gz", "gy", "gx"), P(None, "gz", "gy", "gx")),
        check_vma=False,
    )
```

```python
import jax
import jax.numpy as jnp
from jax import lax
from jax.experimental import pallas as pl
from jax.experimental.pallas import tpu as pltpu
from jax.sharding import PartitionSpec as P

MESH = pl.DeviceIdType.MESH
HIGH = lax.Precision.HIGHEST
SIZES = (4, 8, 32)
GRID_TOTAL = 4194304
STENCIL = (-205.0 / 72.0, 8.0 / 5.0, -1.0 / 5.0, 8.0 / 315.0, -1.0 / 560.0)
KIN = tuple(-0.5 * c for c in STENCIL)
PAIRS = [(i, j) for j in range(4) for i in range(j + 1)]
HALOS = [(0, 0, 1), (0, 0, -1), (0, 1, 0), (0, -1, 0)]
PLANE = sorted(
    [(0, 0, d) for d in range(1, 32)],
    key=lambda delta: -min(delta[2] % 8, 8 - delta[2] % 8) - min(delta[2] // 8, 4 - delta[2] // 8),
)
SIDES = (-1, 0, 1)
HUB = 1
MEMBERS = [c for c in range(32) if c != HUB]


def here():
    return lax.axis_index("gx"), lax.axis_index("gy"), lax.axis_index("gz")


def at_offset(delta):
    return tuple(
        v if d % n == 0 else (v + (d % n)) & (n - 1) for v, d, n in zip(here(), delta, SIZES)
    )


def lanes(shape):
    return lax.broadcasted_iota(jnp.int32, shape, len(shape) - 1)


def sublanes(shape):
    return lax.broadcasted_iota(jnp.int32, shape, len(shape) - 2)


def row_sum(v):
    total = v[0:8]
    for k in range(8, v.shape[0], 8):
        total = total + v[k : k + 8]
    for shift in (4, 2, 1):
        total = total + pltpu.roll(total, shift, 0)
    return total


def main_kernel(
    orb_hbm, pot_hbm, atom_hbm, points_hbm, count, beta_hbm, coup_hbm,
    image_ref, gram_ref,
    psi, pot, pts, beta, coup, atom,
    zb, hy, pk, xcor, msg, a2, row_own, rows16, onehot, spread,
    r1, pe, xc, kr, stage, row_hub, ba, row_all, xrow,
    lsem, hsend, hrecv, csend, crecv,
):
    f32 = jnp.float32
    loads = [
        pltpu.make_async_copy(orb_hbm, psi, lsem.at[0]),
        pltpu.make_async_copy(points_hbm.at[0, 0, 0], pts, lsem.at[1]),
        pltpu.make_async_copy(beta_hbm.at[0, 0, 0], beta, lsem.at[2]),
        pltpu.make_async_copy(atom_hbm, atom, lsem.at[3]),
        pltpu.make_async_copy(coup_hbm, coup, lsem.at[4]),
        pltpu.make_async_copy(pot_hbm, pot, lsem.at[5]),
    ]
    for load in loads:
        load.start()
    x, y, z = here()
    column = x * 8 + y
    is_hub = column == HUB

    def hub_of(d):
        return (0, HUB, (z + d) & 31)

    def member(c, d):
        return (c >> 3, c & 7, (z + d) & 31)

    barrier = pltpu.get_barrier_semaphore()

    def greet(device):
        pl.semaphore_signal(barrier, inc=1, device_id=device, device_id_type=MESH)

    for delta in reversed(HALOS):
        greet(at_offset(delta))
    for d in (-1, 1):
        greet(hub_of(d))

    @pl.when(jnp.logical_not(is_hub))
    def _():
        greet(hub_of(0))

    @pl.when(is_hub)
    def _():
        for d in (-1, 1):
            greet(hub_of(d))

        for c in MEMBERS:
            for d in SIDES:
                greet(member(c, d))
        for d in range(1, 32):
            greet(hub_of(d))

    def remote(src, dst, send, recv, device):
        return pltpu.make_async_remote_copy(
            src_ref=src, dst_ref=dst, send_sem=send, recv_sem=recv,
            device_id=device, device_id_type=MESH,
        )

    def wait_bytes(ref, sem):
        pltpu.make_async_copy(ref, ref, sem).wait()

    lane8, sub8 = lanes((8, 128)), sublanes((8, 128))
    loads[0].wait()

    packed = jnp.zeros((8, 128), f32)
    for n in range(4):
        for zz in range(4):
            g = n * 4 + zz
            moved = pltpu.roll(psi[n, zz], (4 + 8 * g) % 128, 1)
            packed = jnp.where(lane8 // 8 == g, moved, packed)
    pk[...] = packed

    pl.semaphore_wait(barrier, jnp.where(is_hub, 4 + 2 + 2 + 31 * 4, 4 + 3))
    halo_copies = [
        (psi, zb.at[0]),
        (psi, zb.at[1]),
        (psi.at[:, :, pl.ds(4, 4)], hy.at[:, :, pl.ds(4, 4)]),
        (psi.at[:, :, pl.ds(0, 4)], hy.at[:, :, pl.ds(0, 4)]),
    ]
    halos = [
        remote(src, dst, hsend.at[k], hrecv.at[k], at_offset(HALOS[k]))
        for k, (src, dst) in enumerate(halo_copies)
    ]
    for halo in halos:
        halo.start()

    @pl.when(jnp.logical_not(is_hub))
    def _():
        remote(pk, pe.at[column], csend.at[4], crecv.at[4], hub_of(0)).start()

    loads[1].wait()
    lo = [pts[8 * h : 8 * h + 8] & 127 for h in range(2)]
    hi = [pts[8 * h : 8 * h + 8] >> 7 for h in range(2)]
    gathered = [[jnp.zeros((8, 128), f32) for _ in range(2)] for _ in range(4)]
    for row in range(32):
        pick = [hi[h] == row for h in range(2)]
        for n in range(4):
            line = jnp.broadcast_to(psi[n, row // 8, row % 8 : row % 8 + 1], (8, 128))
            for h in range(2):
                got = jnp.take_along_axis(line, lo[h], axis=1)
                gathered[n][h] = jnp.where(pick[h], got, gathered[n][h])

    for load in loads[2:]:
        load.wait()
    slots = count[0, 0, 0]
    dir_of, kind_of = [], []
    for b in range(16):
        a = atom[0, 0, 0, b]
        owner = a // 3
        dx = ((owner & 3) - x + 1) & 3
        dy = (((owner >> 2) & 7) - y + 1) & 7
        dz = ((owner >> 5) - z + 1) & 31
        where = jnp.minimum(jnp.maximum(dz * 16 + dy * 3 + dx, 0), 47)
        dir_of.append(where)
        kind_of.append(a - owner * 3)
    dir_lane = jnp.full((48, 128), 63, jnp.int32)
    for b in range(16):
        used = jnp.where(b < slots, dir_of[b], 63)
        dir_lane = jnp.where(lanes((48, 128)) // 8 == b, used, dir_lane)
    select = (sublanes((48, 128)) == dir_lane).astype(f32)

    lane_n, lane_k, lane_p = lane8 // 32, (lane8 // 8) & 3, lane8 & 7
    blocks = []
    for b in range(16):
        block = jnp.zeros((8, 128), f32)
        for n in range(4):
            line = jnp.broadcast_to(gathered[n][b // 8][b % 8 : b % 8 + 1], (8, 128))
            part = jnp.sum(beta[b] * line, axis=1, keepdims=True)
            block = jnp.where(lane_n == n, part, block)
        keep = (lane_p == sub8) & (lane_k == kind_of[b])
        blocks.append(jnp.where(keep, block, 0.0))
    msg[...] = jnp.dot(
        select, jnp.concatenate(blocks, axis=0), precision=HIGH, preferred_element_type=f32
    )

    def send_rows(d):
        src, dst = msg.at[pl.ds(16 * (d + 1), 9)], r1.at[32 * (d + 1) + column, pl.ds(0, 9)]
        remote(src, dst, csend.at[0], crecv.at[0], hub_of(d)).start()

    send_rows(-1)
    send_rows(1)

    @pl.when(jnp.logical_not(is_hub))
    def _():
        send_rows(0)

    li, si = lanes((128, 128)), sublanes((128, 128))
    away = (li - si) & 127
    away = jnp.minimum(away, 128 - away)
    along_x = jnp.where(away == 0, 3.0 * KIN[0], 0.0)
    for o in range(1, 5):
        along_x = jnp.where(away == o, KIN[o], along_x)
    flat = psi[...].reshape(128, 128)
    base = jnp.dot(flat, along_x, precision=HIGH, preferred_element_type=f32)

    for b in range(16):
        line = jnp.broadcast_to(lo[b // 8][b % 8 : b % 8 + 1], (128, 128))
        onehot[:, pl.ds(b * 128, 128)] = (si == line).astype(jnp.bfloat16)

    for halo in halos:
        halo.wait_recv()
    sums = [None] * len(PAIRS)
    for zz in range(4):
        image = []
        for n in range(4):
            own, other = psi[n, zz], hy[n, zz]
            total = base[(n * 4 + zz) * 8 : (n * 4 + zz) * 8 + 8]
            for o in range(1, 5):
                up = psi[n, zz + o] if zz + o < 4 else zb[1, n, zz + o - 4]
                down = psi[n, zz - o] if zz - o >= 0 else zb[0, n, zz - o + 4]
                before = pltpu.roll(jnp.where(sub8 < 8 - o, own, other), o, 0)
                after = pltpu.roll(jnp.where(sub8 >= o, own, other), 8 - o, 0)
                total = total + KIN[o] * ((up + down) + (before + after))
            total = total + pot[zz] * own
            image.append(total)
            image_ref[n, zz] = total
        for k, (i, j) in enumerate(PAIRS):
            term = psi[i, zz] * image[j]
            sums[k] = term if sums[k] is None else sums[k] + term
    local = jnp.zeros((8, 128), f32)
    for k, (i, j) in enumerate(PAIRS):
        total = jnp.sum(sums[k], axis=1, keepdims=True)
        local = jnp.where(lane8 == j * 32 + (j - i) * 8, total, local)
    row_own[...] = row_sum(local)

    @pl.when(jnp.logical_not(is_hub))
    def _():
        remote(
            row_own.at[pl.ds(0, 1)], kr.at[column, pl.ds(0, 1)], csend.at[5], crecv.at[5], hub_of(0)
        ).start()

    @pl.when(is_hub)
    def _():
        kr[HUB] = row_own[...]
        pe[HUB] = pk[...]
        r1[32 + HUB, pl.ds(0, 9)] = msg[pl.ds(16, 9)]
        sj, lj = si & 7, li & 7
        edge = jnp.zeros((128, 128), f32)
        for o in range(1, 5):
            left = (sj < 4) & (lj >= 4) & (lj - sj == o)
            right = (sj >= 4) & (lj < 4) & (sj - lj == o)
            edge = jnp.where((si // 8 == li // 8) & (left | right), KIN[o], edge)
        tiles = []
        for c in range(2):
            tile = jnp.concatenate([coup[c], jnp.zeros((8, 120), f32)], axis=1)
            for shift in (8, 16, 32, 64):
                tile = tile + pltpu.roll(tile, shift, 1)
            tiles.append(tile)
        couple = jnp.concatenate(
            [jnp.where(lane8 // 8 == r, tiles[0 if r % 4 == 0 else 1], 0.0) for r in range(16)],
            axis=0,
        )

        def reaches(box, c, r):
            third = (r * 11) >> 5
            tx = ((c >> 3) + (r - 3 * third) + 3) & 3
            ty = ((c & 7) + third + 7) & 7
            return ((r < 9) & (box == tx * 8 + ty)).astype(f32)

        col, box = lanes((32, 512)), sublanes((32, 512))
        collect = reaches(box, col >> 4, col & 15)
        row, box = sublanes((512, 32)), lanes((512, 32))
        spread_out = reaches(box, row >> 4, row & 15)

        wait_bytes(pe.at[pl.ds(0, 31)], crecv.at[4])
        edges = []
        for c in range(32):
            before, after = (c + 24) % 32, (c + 8) % 32
            edges.append(jnp.where(lane8 & 7 < 4, pe[before], pe[after]) - pe[c])
        change = jnp.dot(
            jnp.concatenate(edges, axis=0), edge, precision=HIGH, preferred_element_type=f32
        )
        outer = [jnp.zeros((8, 128), f32) for _ in range(4)]
        for c in range(32):
            part = change[8 * c : 8 * c + 8]
            xc[c] = part
            for s in range(4):
                outer[s] = outer[s] + (pltpu.roll(pe[c], 32 * s, 1) if s else pe[c]) * part

        wait_bytes(r1.at[pl.ds(0, 95), pl.ds(0, 9)], crecv.at[0])
        gathered_rows = (r1[pl.ds(0, 32)] + r1[pl.ds(64, 32)]) + r1[pl.ds(32, 32)]
        gathered_rows = jnp.where(sublanes((32, 16, 128)) < 9, gathered_rows, 0.0)
        coef = jnp.dot(
            collect, gathered_rows.reshape(512, 128), precision=HIGH, preferred_element_type=f32
        )
        applied = jnp.dot(coef, couple, precision=HIGH, preferred_element_type=f32)

        def hand_out(c, d):
            remote(
                stage.at[c, pl.ds(0, 9)], a2.at[pl.ds(16 * (1 - d), 9)], csend.at[1], crecv.at[1],
                member(c, d),
            ).start()

        for v in range(4):
            c8, a8 = coef[8 * v : 8 * v + 8], applied[8 * v : 8 * v + 8]
            for s in range(4):
                outer[s] = outer[s] + (pltpu.roll(c8, 32 * s, 1) if s else c8) * a8
        placed = jnp.zeros((8, 128), f32)
        for s in range(4):
            part = outer[s]
            part = (part + pltpu.roll(part, 120, 1)) + (pltpu.roll(part, 112, 1) + pltpu.roll(part, 104, 1))
            part = jnp.where(lane8 & 31 < 8, part, 0.0)
            placed = placed + (pltpu.roll(part, 8 * s, 1) if s else part)
        placed = row_sum(placed)
        wait_bytes(kr.at[pl.ds(0, 31), pl.ds(0, 1)], crecv.at[5])
        kinetic = kr[0]
        for c in range(1, 32):
            kinetic = kinetic + kr[c]
        row_hub[...] = placed + kinetic
        ba[pl.ds(31, 1)] = row_hub[pl.ds(0, 1)]
        for k, delta in enumerate(PLANE):
            remote(
                row_hub.at[pl.ds(0, 1)], ba.at[pl.ds(k, 1)], csend.at[2], crecv.at[2], at_offset(delta)
            ).start()
        stage[...] = jnp.dot(
            spread_out, applied, precision=HIGH, preferred_element_type=f32
        ).reshape(32, 16, 128)
        hand_out(HUB, -1)
        hand_out(HUB, 1)
        for c in MEMBERS:
            for d in SIDES:
                hand_out(c, d)
            remote(xc.at[c], xcor, csend.at[6], crecv.at[6], member(c, 0)).start()
        a2[pl.ds(16, 9)] = stage[HUB, pl.ds(0, 9)]
        xcor[...] = xc[HUB]

    @pl.when(is_hub)
    def _():
        wait_bytes(a2.at[pl.ds(0, 18)], crecv.at[1])

    @pl.when(jnp.logical_not(is_hub))
    def _():
        wait_bytes(a2.at[pl.ds(0, 27)], crecv.at[1])
        wait_bytes(xcor, crecv.at[6])

    for b in range(16):
        rows16[pl.ds(b, 1)] = a2[pl.ds(dir_of[b], 1)]
    spots = []
    for h in range(2):
        kind = jnp.zeros((8, 128), jnp.int32)
        for b in range(8):
            kind = jnp.where(sub8 == b, kind_of[h * 8 + b], kind)
        spots.append(kind * 8 + lane_p)
    left = []
    for n in range(4):
        for h in range(2):
            got = jnp.take_along_axis(rows16[pl.ds(h * 8, 8)], spots[h] + 32 * n, axis=1)
            slot = sub8 + 8 * h
            left.append(jnp.where((lane8 // 8 == slot) & (slot < slots), got, 0.0))
    values = jnp.dot(
        jnp.concatenate(left, axis=0), beta[...].reshape(128, 128), precision=HIGH,
        preferred_element_type=f32,
    )
    high = values.astype(jnp.bfloat16).astype(f32)
    low = values - high
    for b in range(16):
        line = jnp.broadcast_to(hi[b // 8][b % 8 : b % 8 + 1], (32, 128))
        pick = sublanes((32, 128)) == line
        for part, source in enumerate((high, low)):
            for n in range(4):
                r = n * 16 + b
                piece = jnp.where(pick, jnp.broadcast_to(source[r : r + 1], (32, 128)), 0.0)
                spread[pl.ds(part * 128 + n * 32, 32), pl.ds(b * 128, 128)] = piece.astype(jnp.bfloat16)
    grid = lax.dot_general(
        spread[...], onehot[...], (((1,), (1,)), ((), ())), preferred_element_type=f32
    )
    at_edge = (lane8 < 4) | (lane8 >= 124)
    for n in range(4):
        for zz in range(4):
            g = n * 4 + zz
            moved = pltpu.roll(xcor[...], (124 - 8 * g) % 128, 1)
            projected = grid[8 * g : 8 * g + 8] + grid[128 + 8 * g : 136 + 8 * g]
            image_ref[n, zz] = image_ref[n, zz] + jnp.where(at_edge, moved, 0.0) + projected

    @pl.when(is_hub)
    def _():
        wait_bytes(ba.at[pl.ds(0, 31)], crecv.at[2])
        row_all[...] = row_sum(ba[...])

        for c in MEMBERS:
            row = row_all.at[pl.ds(0, 1)]
            remote(row, xrow.at[pl.ds(0, 1)], csend.at[3], crecv.at[3], member(c, 0)).start()
        gram_ref[...] = row_all[...]
        wait_bytes(msg.at[pl.ds(0, 18)], csend.at[0])
        wait_bytes(r1.at[pl.ds(0, 95), pl.ds(0, 9)], csend.at[1])
        wait_bytes(pe.at[pl.ds(0, 31)], csend.at[6])
        wait_bytes(ba.at[pl.ds(0, 31)], csend.at[2])
        wait_bytes(kr.at[pl.ds(0, 31), pl.ds(0, 1)], csend.at[3])

    @pl.when(jnp.logical_not(is_hub))
    def _():
        wait_bytes(xrow.at[pl.ds(0, 1)], crecv.at[3])
        gram_ref[...] = jnp.broadcast_to(xrow[pl.ds(0, 1)], (8, 128))
        wait_bytes(msg.at[pl.ds(0, 27)], csend.at[0])
        wait_bytes(pk, csend.at[4])
        wait_bytes(row_own.at[pl.ds(0, 1)], csend.at[5])

    for halo in halos:
        halo.wait_send()


def residual_kernel(psi, image, gram, image_out, residual_out, residual, sem):
    copies = [pltpu.make_async_copy(image, image_out, sem.at[4])]
    copies[0].start()
    lane8 = lanes((8, 128))
    row = gram[...]
    weight = {}
    for i, j in PAIRS:
        group = j * 4 + (j - i)
        total = jnp.sum(jnp.where(lane8 // 8 == group, row, 0.0), axis=1, keepdims=True)
        total = jnp.broadcast_to(total, (8, 128)) * (1.0 / GRID_TOTAL)
        weight[i, j] = weight[j, i] = total
    for j in range(4):
        for z in range(4):
            total = image[j, z]
            for i in range(4):
                total = total - weight[i, j] * psi[i, z]
            residual[j, z] = total
        copies.append(pltpu.make_async_copy(residual.at[j], residual_out.at[j], sem.at[j]))
        copies[-1].start()
    for copy in copies:
        copy.wait()


def on_device(orbitals, potential, block_atom, block_points, block_count, projector_values, coupling):
    f32, i32 = jnp.float32, jnp.int32
    hbm = pl.BlockSpec(memory_space=pl.ANY)
    vmem = pl.BlockSpec(memory_space=pltpu.VMEM)
    field = jax.ShapeDtypeStruct((4, 4, 8, 128), f32)
    held = [
        pltpu.with_memory_space_constraint(v, pltpu.HBM)
        for v in (orbitals, potential, block_atom, block_points, projector_values, coupling)
    ]
    held.insert(4, block_count)
    image, gram = pl.pallas_call(
        main_kernel,
        out_shape=(pltpu.VMEM((4, 4, 8, 128), f32), pltpu.VMEM((8, 128), f32)),
        in_specs=[hbm] * 4 + [pl.BlockSpec(memory_space=pltpu.SMEM)] + [hbm] * 2,
        out_specs=(vmem, vmem),
        scratch_shapes=[
            pltpu.VMEM((4, 4, 8, 128), f32),
            pltpu.VMEM((4, 8, 128), f32),
            pltpu.VMEM((16, 128), i32),
            pltpu.VMEM((16, 8, 128), f32),
            pltpu.VMEM((2, 8, 8), f32),
            pltpu.SMEM((1, 1, 1, 16), i32),
            pltpu.VMEM((2, 4, 4, 8, 128), f32),
            pltpu.VMEM((4, 4, 8, 128), f32),
            pltpu.VMEM((8, 128), f32),
            pltpu.VMEM((8, 128), f32),
            pltpu.VMEM((48, 128), f32),
            pltpu.VMEM((48, 128), f32),
            pltpu.VMEM((8, 128), f32),
            pltpu.VMEM((16, 128), f32),
            pltpu.VMEM((128, 2048), jnp.bfloat16),
            pltpu.VMEM((256, 2048), jnp.bfloat16),
            pltpu.VMEM((96, 16, 128), f32),
            pltpu.VMEM((32, 8, 128), f32),
            pltpu.VMEM((32, 8, 128), f32),
            pltpu.VMEM((32, 8, 128), f32),
            pltpu.VMEM((32, 16, 128), f32),
            pltpu.VMEM((8, 128), f32),
            pltpu.VMEM((32, 128), f32),
            pltpu.VMEM((8, 128), f32),
            pltpu.VMEM((8, 128), f32),
            pltpu.SemaphoreType.DMA((6,)),
            pltpu.SemaphoreType.DMA((4,)),
            pltpu.SemaphoreType.DMA((4,)),
            pltpu.SemaphoreType.DMA((7,)),
            pltpu.SemaphoreType.DMA((7,)),
        ],
        compiler_params=pltpu.CompilerParams(
            collective_id=0, has_side_effects=True, vmem_limit_bytes=24 * 1024 * 1024
        ),
    )(*held)
    return pl.pallas_call(
        residual_kernel,
        out_shape=(field, field),
        in_specs=[vmem] * 3,
        out_specs=(hbm, hbm),
        scratch_shapes=[pltpu.VMEM((4, 4, 8, 128), f32), pltpu.SemaphoreType.DMA((5,))],
        compiler_params=pltpu.CompilerParams(vmem_limit_bytes=16 * 1024 * 1024),
    )(orbitals, image, gram)


def solution(mesh):
    return jax.shard_map(
        on_device,
        mesh=mesh,
        in_specs=(
            P(None, "gz", "gy", "gx"),
            P("gz", "gy", "gx"),
            P("gz", "gy", "gx", None),
            P("gz", "gy", "gx", None, None),
            P("gz", "gy", "gx"),
            P("gz", "gy", "gx", None, None, None),
            P(),
        ),
        out_specs=(P(None, "gz", "gy", "gx"), P(None, "gz", "gy", "gx")),
        check_vma=False,
    )
```

```python
import jax
import jax.numpy as jnp
from jax import lax
from jax.experimental import pallas as pl
from jax.experimental.pallas import tpu as pltpu
from jax.sharding import PartitionSpec as P

MESH = pl.DeviceIdType.MESH
HIGH = lax.Precision.HIGHEST
SIZES = (4, 8, 32)
GRID_TOTAL = 4194304
STENCIL = (-205.0 / 72.0, 8.0 / 5.0, -1.0 / 5.0, 8.0 / 315.0, -1.0 / 560.0)
KIN = tuple(-0.5 * c for c in STENCIL)
PAIRS = [(i, j) for j in range(4) for i in range(j + 1)]
UP, DOWN = (0, 0, 1), (0, 0, -1)
HALOS = [UP, DOWN, (0, 1, 0), (0, -1, 0), UP, DOWN]
PLANE = sorted(
    [(0, 0, d) for d in range(1, 32)],
    key=lambda delta: -min(delta[2] % 8, 8 - delta[2] % 8) - min(delta[2] // 8, 4 - delta[2] // 8),
)
SIDES = (-1, 0, 1)
HUB = 1
MEMBERS = [c for c in range(32) if c != HUB]


def here():
    return lax.axis_index("gx"), lax.axis_index("gy"), lax.axis_index("gz")


def at_offset(delta):
    return tuple(
        v if d % n == 0 else (v + (d % n)) & (n - 1) for v, d, n in zip(here(), delta, SIZES)
    )


def lanes(shape):
    return lax.broadcasted_iota(jnp.int32, shape, len(shape) - 1)


def sublanes(shape):
    return lax.broadcasted_iota(jnp.int32, shape, len(shape) - 2)


def row_sum(v):
    total = v[0:8]
    for k in range(8, v.shape[0], 8):
        total = total + v[k : k + 8]
    for shift in (4, 2, 1):
        total = total + pltpu.roll(total, shift, 0)
    return total


def main_kernel(
    orb_hbm, pot_hbm, atom_hbm, points_hbm, count, beta_hbm, coup_hbm,
    image_ref, gram_ref,
    psi, pot, pts, beta, coup, atom,
    zb, hy, pk, msg, a2, row_own, rows16, onehot, spread,
    r1, pe, kr, stage, row_hub, ba, row_all, xrow, sent,
    lsem, hsend, hrecv, csend, crecv,
):
    f32 = jnp.float32
    loads = [
        pltpu.make_async_copy(orb_hbm, psi, lsem.at[0]),
        pltpu.make_async_copy(points_hbm.at[0, 0, 0], pts, lsem.at[1]),
        pltpu.make_async_copy(beta_hbm.at[0, 0, 0], beta, lsem.at[2]),
        pltpu.make_async_copy(atom_hbm, atom, lsem.at[3]),
        pltpu.make_async_copy(coup_hbm, coup, lsem.at[4]),
        pltpu.make_async_copy(pot_hbm, pot, lsem.at[5]),
    ]
    for load in loads:
        load.start()
    x, y, z = here()
    column = x * 8 + y
    is_hub = column == HUB

    def hub_of(d):
        return (0, HUB, (z + d) & 31)

    def member(c, d):
        return (c >> 3, c & 7, (z + d) & 31)

    barrier = pltpu.get_barrier_semaphore()

    def greet(device):
        pl.semaphore_signal(barrier, inc=1, device_id=device, device_id_type=MESH)

    for delta in reversed(HALOS[:4]):
        greet(at_offset(delta))
    for d in (-1, 1):
        greet(hub_of(d))

    @pl.when(jnp.logical_not(is_hub))
    def _():
        greet(hub_of(0))

    @pl.when(is_hub)
    def _():
        for d in (-1, 1):
            greet(hub_of(d))

        for c in MEMBERS:
            for d in SIDES:
                greet(member(c, d))
        for d in range(1, 32):
            greet(hub_of(d))

    def remote(src, dst, send, recv, device):
        return pltpu.make_async_remote_copy(
            src_ref=src, dst_ref=dst, send_sem=send, recv_sem=recv,
            device_id=device, device_id_type=MESH,
        )

    def wait_bytes(ref, sem):
        pltpu.make_async_copy(ref, ref, sem).wait()

    lane8, sub8 = lanes((8, 128)), sublanes((8, 128))
    loads[0].wait()

    packed = jnp.zeros((8, 128), f32)
    for n in range(4):
        for zz in range(4):
            g = n * 4 + zz
            moved = pltpu.roll(psi[n, zz], (4 + 8 * g) % 128, 1)
            packed = jnp.where(lane8 // 8 == g, moved, packed)
    pk[...] = packed

    pl.semaphore_wait(barrier, jnp.where(is_hub, 4 + 2 + 2 + 31 * 4, 4 + 3))
    halo_copies = [
        (psi.at[:, pl.ds(2, 2)], zb.at[0, :, pl.ds(2, 2)]),
        (psi.at[:, pl.ds(0, 2)], zb.at[1, :, pl.ds(0, 2)]),
        (psi.at[:, :, pl.ds(4, 4)], hy.at[:, :, pl.ds(4, 4)]),
        (psi.at[:, :, pl.ds(0, 4)], hy.at[:, :, pl.ds(0, 4)]),
        (psi.at[:, pl.ds(0, 2)], zb.at[0, :, pl.ds(0, 2)]),
        (psi.at[:, pl.ds(2, 2)], zb.at[1, :, pl.ds(2, 2)]),
    ]
    halos = [
        remote(src, dst, hsend.at[k], hrecv.at[k], at_offset(HALOS[k]))
        for k, (src, dst) in enumerate(halo_copies)
    ]
    for halo in halos[:4]:
        halo.start()

    @pl.when(jnp.logical_not(is_hub))
    def _():
        remote(pk, pe.at[column], csend.at[4], crecv.at[4], hub_of(0)).start()

    loads[1].wait()
    lo = [pts[8 * h : 8 * h + 8] & 127 for h in range(2)]
    hi = [pts[8 * h : 8 * h + 8] >> 7 for h in range(2)]
    gathered = [[jnp.zeros((8, 128), f32) for _ in range(2)] for _ in range(4)]
    for row in range(32):
        pick = [hi[h] == row for h in range(2)]
        for n in range(4):
            line = jnp.broadcast_to(psi[n, row // 8, row % 8 : row % 8 + 1], (8, 128))
            for h in range(2):
                got = jnp.take_along_axis(line, lo[h], axis=1)
                gathered[n][h] = jnp.where(pick[h], got, gathered[n][h])

    for load in loads[2:]:
        load.wait()
    slots = count[0, 0, 0]
    dir_of, back_of, kind_of = [], [], []
    for b in range(16):
        a = atom[0, 0, 0, b]
        owner = a // 3
        dx = ((owner & 3) - x + 1) & 3
        dy = (((owner >> 2) & 7) - y + 1) & 7
        dz = ((owner >> 5) - z + 1) & 31
        where = jnp.minimum(jnp.maximum(dz * 16 + dy * 3 + dx, 0), 47)
        back = jnp.minimum(jnp.maximum(dz * 24 + dy * 3 + dx + 8, 0), 71)
        dir_of.append(where)
        back_of.append(back)
        kind_of.append(a - owner * 3)
    dir_lane = jnp.full((48, 128), 63, jnp.int32)
    for b in range(16):
        used = jnp.where(b < slots, dir_of[b], 63)
        dir_lane = jnp.where(lanes((48, 128)) // 8 == b, used, dir_lane)
    select = (sublanes((48, 128)) == dir_lane).astype(f32)

    lane_n, lane_k, lane_p = lane8 // 32, (lane8 // 8) & 3, lane8 & 7
    blocks = []
    for b in range(16):
        block = jnp.zeros((8, 128), f32)
        for n in range(4):
            line = jnp.broadcast_to(gathered[n][b // 8][b % 8 : b % 8 + 1], (8, 128))
            part = jnp.sum(beta[b] * line, axis=1, keepdims=True)
            block = jnp.where(lane_n == n, part, block)
        keep = (lane_p == sub8) & (lane_k == kind_of[b])
        blocks.append(jnp.where(keep, block, 0.0))
    msg[...] = jnp.dot(
        select, jnp.concatenate(blocks, axis=0), precision=HIGH, preferred_element_type=f32
    )

    def send_rows(d):
        src, dst = msg.at[pl.ds(16 * (d + 1), 9)], r1.at[32 * (d + 1) + column, pl.ds(0, 9)]
        remote(src, dst, csend.at[0], crecv.at[0], hub_of(d)).start()

    send_rows(-1)
    send_rows(1)

    @pl.when(jnp.logical_not(is_hub))
    def _():
        send_rows(0)

    for halo in halos[4:]:
        halo.start()

    li, si = lanes((128, 128)), sublanes((128, 128))
    away = (li - si) & 127
    away = jnp.minimum(away, 128 - away)
    along_x = jnp.where(away == 0, 3.0 * KIN[0], 0.0)
    for o in range(1, 5):
        along_x = jnp.where(away == o, KIN[o], along_x)
    flat = psi[...].reshape(128, 128)
    base = jnp.dot(flat, along_x, precision=HIGH, preferred_element_type=f32)

    for b in range(16):
        line = jnp.broadcast_to(lo[b // 8][b % 8 : b % 8 + 1], (128, 128))
        onehot[:, pl.ds(b * 128, 128)] = (si == line).astype(jnp.bfloat16)

    halos[2].wait_recv()
    halos[3].wait_recv()
    sums = [None] * len(PAIRS)
    for zz in range(4):
        image = []
        for n in range(4):
            own, other = psi[n, zz], hy[n, zz]
            total = base[(n * 4 + zz) * 8 : (n * 4 + zz) * 8 + 8]
            for o in range(1, 5):
                before = pltpu.roll(jnp.where(sub8 < 8 - o, own, other), o, 0)
                after = pltpu.roll(jnp.where(sub8 >= o, own, other), 8 - o, 0)
                near = before + after
                if zz + o < 4:
                    near = near + psi[n, zz + o]
                if zz - o >= 0:
                    near = near + psi[n, zz - o]
                total = total + KIN[o] * near
            total = total + pot[zz] * own
            image.append(total)
            image_ref[n, zz] = total
        for k, (i, j) in enumerate(PAIRS):
            term = psi[i, zz] * image[j]
            sums[k] = term if sums[k] is None else sums[k] + term
    halos[0].wait_recv()
    halos[1].wait_recv()
    for zz in range(4):
        cross = []
        for n in range(4):
            total = KIN[4 - zz] * zb[1, n, 0]
            if zz >= 1:
                total = total + KIN[5 - zz] * zb[1, n, 1]
            for layer in (2, 3):
                if zz >= 2 and layer >= zz:
                    total = total + KIN[4 + zz - layer] * zb[0, n, layer]
            cross.append(total)
        for k, (i, j) in enumerate(PAIRS):
            sums[k] = sums[k] + (psi[i, zz] * cross[j] + psi[j, zz] * cross[i])
    local = jnp.zeros((8, 128), f32)
    for k, (i, j) in enumerate(PAIRS):
        total = jnp.sum(sums[k], axis=1, keepdims=True)
        local = jnp.where(lane8 == j * 32 + (j - i) * 8, total, local)
    row_own[...] = row_sum(local)

    @pl.when(jnp.logical_not(is_hub))
    def _():
        remote(
            row_own.at[pl.ds(0, 1)], kr.at[column, pl.ds(0, 1)], csend.at[5], crecv.at[5], hub_of(0)
        ).start()

    @pl.when(is_hub)
    def _():
        kr[HUB] = row_own[...]
        pe[HUB] = pk[...]
        r1[32 + HUB, pl.ds(0, 9)] = msg[pl.ds(16, 9)]
        sj, lj = si & 7, li & 7
        edge = jnp.zeros((128, 128), f32)
        for o in range(1, 5):
            left = (sj < 4) & (lj >= 4) & (lj - sj == o)
            right = (sj >= 4) & (lj < 4) & (sj - lj == o)
            edge = jnp.where((si // 8 == li // 8) & (left | right), KIN[o], edge)
        tiles = []
        for c in range(2):
            tile = jnp.concatenate([coup[c], jnp.zeros((8, 120), f32)], axis=1)
            for shift in (8, 16, 32, 64):
                tile = tile + pltpu.roll(tile, shift, 1)
            tiles.append(tile)
        couple = jnp.concatenate(
            [jnp.where(lane8 // 8 == r, tiles[0 if r % 4 == 0 else 1], 0.0) for r in range(16)],
            axis=0,
        )

        def reaches(box, c, r):
            third = (r * 11) >> 5
            tx = ((c >> 3) + (r - 3 * third) + 3) & 3
            ty = ((c & 7) + third + 7) & 7
            return ((r < 9) & (box == tx * 8 + ty)).astype(f32)

        col, box = lanes((32, 512)), sublanes((32, 512))
        collect = reaches(box, col >> 4, col & 15)
        row, box = sublanes((512, 32)), lanes((512, 32))
        spread_out = reaches(box, row >> 4, row & 15)

        wait_bytes(pe.at[pl.ds(0, 31)], crecv.at[4])
        edges = []
        for c in range(32):
            before, after = (c + 24) % 32, (c + 8) % 32
            edges.append(jnp.where(lane8 & 7 < 4, pe[before], pe[after]) - pe[c])
        change = jnp.dot(
            jnp.concatenate(edges, axis=0), edge, precision=HIGH, preferred_element_type=f32
        )
        outer = [jnp.zeros((8, 128), f32) for _ in range(4)]
        for c in range(32):
            part = change[8 * c : 8 * c + 8]
            stage[c, pl.ds(0, 8)] = part
            for s in range(4):
                outer[s] = outer[s] + (pltpu.roll(pe[c], 32 * s, 1) if s else pe[c]) * part

        wait_bytes(r1.at[pl.ds(0, 95), pl.ds(0, 9)], crecv.at[0])
        gathered_rows = (r1[pl.ds(0, 32)] + r1[pl.ds(64, 32)]) + r1[pl.ds(32, 32)]
        gathered_rows = jnp.where(sublanes((32, 16, 128)) < 9, gathered_rows, 0.0)
        coef = jnp.dot(
            collect, gathered_rows.reshape(512, 128), precision=HIGH, preferred_element_type=f32
        )
        applied = jnp.dot(coef, couple, precision=HIGH, preferred_element_type=f32)

        stage[:, pl.ds(8, 16)] = jnp.dot(
            spread_out, applied, precision=HIGH, preferred_element_type=f32
        ).reshape(32, 16, 128)

        def hand_out(c, d):
            first, rows = (0, 17) if d == 0 else (8, 9)
            remote(
                stage.at[c, pl.ds(first, rows)], a2.at[pl.ds(24 * (1 - d) + first, rows)],
                csend.at[1], crecv.at[1], member(c, d),
            ).start()

        hand_out(HUB, -1)
        hand_out(HUB, 1)
        a2[pl.ds(24, 17)] = stage[HUB, pl.ds(0, 17)]
        for v in range(4):
            c8, a8 = coef[8 * v : 8 * v + 8], applied[8 * v : 8 * v + 8]
            for s in range(4):
                outer[s] = outer[s] + (pltpu.roll(c8, 32 * s, 1) if s else c8) * a8
        placed = jnp.zeros((8, 128), f32)
        for s in range(4):
            part = outer[s]
            part = (part + pltpu.roll(part, 120, 1)) + (pltpu.roll(part, 112, 1) + pltpu.roll(part, 104, 1))
            part = jnp.where(lane8 & 31 < 8, part, 0.0)
            placed = placed + (pltpu.roll(part, 8 * s, 1) if s else part)
        placed = row_sum(placed)
        wait_bytes(kr.at[pl.ds(0, 31), pl.ds(0, 1)], crecv.at[5])
        kinetic = kr[0]
        for c in range(1, 32):
            kinetic = kinetic + kr[c]
        row_hub[...] = placed + kinetic
        ba[pl.ds(31, 1)] = row_hub[pl.ds(0, 1)]
        for k, delta in enumerate(PLANE):
            remote(
                row_hub.at[pl.ds(0, 1)], ba.at[pl.ds(k, 1)], csend.at[2], crecv.at[2], at_offset(delta)
            ).start()
        for c in MEMBERS:
            for d in SIDES:
                hand_out(c, d)

    @pl.when(is_hub)
    def _():
        wait_bytes(a2.at[pl.ds(0, 18)], crecv.at[1])

    @pl.when(jnp.logical_not(is_hub))
    def _():
        wait_bytes(a2.at[pl.ds(0, 35)], crecv.at[1])

    halos[4].wait_recv()
    halos[5].wait_recv()
    for b in range(16):
        rows16[pl.ds(b, 1)] = a2[pl.ds(back_of[b], 1)]
    spots = []
    for h in range(2):
        kind = jnp.zeros((8, 128), jnp.int32)
        for b in range(8):
            kind = jnp.where(sub8 == b, kind_of[h * 8 + b], kind)
        spots.append(kind * 8 + lane_p)
    left = []
    for n in range(4):
        for h in range(2):
            got = jnp.take_along_axis(rows16[pl.ds(h * 8, 8)], spots[h] + 32 * n, axis=1)
            slot = sub8 + 8 * h
            left.append(jnp.where((lane8 // 8 == slot) & (slot < slots), got, 0.0))
    values = jnp.dot(
        jnp.concatenate(left, axis=0), beta[...].reshape(128, 128), precision=HIGH,
        preferred_element_type=f32,
    )
    high = values.astype(jnp.bfloat16).astype(f32)
    low = values - high
    for b in range(16):
        line = jnp.broadcast_to(hi[b // 8][b % 8 : b % 8 + 1], (32, 128))
        pick = sublanes((32, 128)) == line
        for part, source in enumerate((high, low)):
            for n in range(4):
                r = n * 16 + b
                piece = jnp.where(pick, jnp.broadcast_to(source[r : r + 1], (32, 128)), 0.0)
                spread[pl.ds(part * 128 + n * 32, 32), pl.ds(b * 128, 128)] = piece.astype(jnp.bfloat16)
    grid = lax.dot_general(
        spread[...], onehot[...], (((1,), (1,)), ((), ())), preferred_element_type=f32
    )
    at_edge = (lane8 < 4) | (lane8 >= 124)
    for n in range(4):
        for zz in range(4):
            g = n * 4 + zz
            moved = pltpu.roll(a2[pl.ds(24, 8)], (124 - 8 * g) % 128, 1)
            projected = grid[8 * g : 8 * g + 8] + grid[128 + 8 * g : 136 + 8 * g]
            total = image_ref[n, zz] + jnp.where(at_edge, moved, 0.0)
            for o in range(1, 5):
                if zz + o >= 4:
                    total = total + KIN[o] * zb[1, n, zz + o - 4]
                if zz - o < 0:
                    total = total + KIN[o] * zb[0, n, zz - o + 4]
            image_ref[n, zz] = total + projected

    @pl.when(is_hub)
    def _():
        wait_bytes(ba.at[pl.ds(0, 31)], crecv.at[2])
        row_all[...] = row_sum(ba[...])

        for c in MEMBERS:
            row = row_all.at[pl.ds(0, 1)]
            remote(row, xrow.at[pl.ds(0, 1)], csend.at[3], crecv.at[3], member(c, 0)).start()
        gram_ref[...] = row_all[...]
        wait_bytes(msg.at[pl.ds(0, 18)], csend.at[0])
        wait_bytes(sent.at[pl.ds(0, 95 * 9 + 31 * 8)], csend.at[1])
        wait_bytes(ba.at[pl.ds(0, 31)], csend.at[2])
        wait_bytes(kr.at[pl.ds(0, 31), pl.ds(0, 1)], csend.at[3])

    @pl.when(jnp.logical_not(is_hub))
    def _():
        wait_bytes(xrow.at[pl.ds(0, 1)], crecv.at[3])
        gram_ref[...] = jnp.broadcast_to(xrow[pl.ds(0, 1)], (8, 128))
        wait_bytes(msg.at[pl.ds(0, 27)], csend.at[0])
        wait_bytes(pk, csend.at[4])
        wait_bytes(row_own.at[pl.ds(0, 1)], csend.at[5])

    for halo in halos:
        halo.wait_send()


def residual_kernel(psi, image, gram, image_out, residual_out, residual, sem):
    copies = [pltpu.make_async_copy(image, image_out, sem.at[4])]
    copies[0].start()
    lane8 = lanes((8, 128))
    row = gram[...]
    weight = {}
    for i, j in PAIRS:
        group = j * 4 + (j - i)
        total = jnp.sum(jnp.where(lane8 // 8 == group, row, 0.0), axis=1, keepdims=True)
        total = jnp.broadcast_to(total, (8, 128)) * (1.0 / GRID_TOTAL)
        weight[i, j] = weight[j, i] = total
    for j in range(4):
        for z in range(4):
            total = image[j, z]
            for i in range(4):
                total = total - weight[i, j] * psi[i, z]
            residual[j, z] = total
        copies.append(pltpu.make_async_copy(residual.at[j], residual_out.at[j], sem.at[j]))
        copies[-1].start()
    for copy in copies:
        copy.wait()


def on_device(orbitals, potential, block_atom, block_points, block_count, projector_values, coupling):
    f32, i32 = jnp.float32, jnp.int32
    hbm = pl.BlockSpec(memory_space=pl.ANY)
    vmem = pl.BlockSpec(memory_space=pltpu.VMEM)
    field = jax.ShapeDtypeStruct((4, 4, 8, 128), f32)
    held = [
        pltpu.with_memory_space_constraint(v, pltpu.HBM)
        for v in (orbitals, potential, block_atom, block_points, projector_values, coupling)
    ]
    held.insert(4, block_count)
    image, gram = pl.pallas_call(
        main_kernel,
        out_shape=(pltpu.VMEM((4, 4, 8, 128), f32), pltpu.VMEM((8, 128), f32)),
        in_specs=[hbm] * 4 + [pl.BlockSpec(memory_space=pltpu.SMEM)] + [hbm] * 2,
        out_specs=(vmem, vmem),
        scratch_shapes=[
            pltpu.VMEM((4, 4, 8, 128), f32),
            pltpu.VMEM((4, 8, 128), f32),
            pltpu.VMEM((16, 128), i32),
            pltpu.VMEM((16, 8, 128), f32),
            pltpu.VMEM((2, 8, 8), f32),
            pltpu.SMEM((1, 1, 1, 16), i32),
            pltpu.VMEM((2, 4, 4, 8, 128), f32),
            pltpu.VMEM((4, 4, 8, 128), f32),
            pltpu.VMEM((8, 128), f32),
            pltpu.VMEM((48, 128), f32),
            pltpu.VMEM((72, 128), f32),
            pltpu.VMEM((8, 128), f32),
            pltpu.VMEM((16, 128), f32),
            pltpu.VMEM((128, 2048), jnp.bfloat16),
            pltpu.VMEM((256, 2048), jnp.bfloat16),
            pltpu.VMEM((96, 16, 128), f32),
            pltpu.VMEM((32, 8, 128), f32),
            pltpu.VMEM((32, 8, 128), f32),
            pltpu.VMEM((32, 24, 128), f32),
            pltpu.VMEM((8, 128), f32),
            pltpu.VMEM((32, 128), f32),
            pltpu.VMEM((8, 128), f32),
            pltpu.VMEM((8, 128), f32),
            pltpu.VMEM((1104, 128), f32),
            pltpu.SemaphoreType.DMA((6,)),
            pltpu.SemaphoreType.DMA((6,)),
            pltpu.SemaphoreType.DMA((6,)),
            pltpu.SemaphoreType.DMA((6,)),
            pltpu.SemaphoreType.DMA((6,)),
        ],
        compiler_params=pltpu.CompilerParams(
            collective_id=0, has_side_effects=True, vmem_limit_bytes=24 * 1024 * 1024
        ),
    )(*held)
    return pl.pallas_call(
        residual_kernel,
        out_shape=(field, field),
        in_specs=[vmem] * 3,
        out_specs=(hbm, hbm),
        scratch_shapes=[pltpu.VMEM((4, 4, 8, 128), f32), pltpu.SemaphoreType.DMA((5,))],
        compiler_params=pltpu.CompilerParams(vmem_limit_bytes=16 * 1024 * 1024),
    )(orbitals, image, gram)


def solution(mesh):
    return jax.shard_map(
        on_device,
        mesh=mesh,
        in_specs=(
            P(None, "gz", "gy", "gx"),
            P("gz", "gy", "gx"),
            P("gz", "gy", "gx", None),
            P("gz", "gy", "gx", None, None),
            P("gz", "gy", "gx"),
            P("gz", "gy", "gx", None, None, None),
            P(),
        ),
        out_specs=(P(None, "gz", "gy", "gx"), P(None, "gz", "gy", "gx")),
        check_vma=False,
    )
```

```python
import jax
import jax.numpy as jnp
from jax import lax
from jax.experimental import pallas as pl
from jax.experimental.pallas import tpu as pltpu
from jax.sharding import PartitionSpec as P

MESH = pl.DeviceIdType.MESH
HIGH = lax.Precision.HIGHEST
SIZES = (4, 8, 32)
GRID_TOTAL = 4194304
STENCIL = (-205.0 / 72.0, 8.0 / 5.0, -1.0 / 5.0, 8.0 / 315.0, -1.0 / 560.0)
KIN = tuple(-0.5 * c for c in STENCIL)
PAIRS = [(i, j) for j in range(4) for i in range(j + 1)]
UP, DOWN = (0, 0, 1), (0, 0, -1)
HALOS = [UP, DOWN, (0, 1, 0), (0, -1, 0), UP, DOWN]
PLANE = sorted(
    [(0, 0, d) for d in range(1, 32)],
    key=lambda delta: -min(delta[2] % 8, 8 - delta[2] % 8) - min(delta[2] // 8, 4 - delta[2] // 8),
)
SIDES = (-1, 0, 1)
HUB = 1
MEMBERS = [c for c in range(32) if c != HUB]


def here():
    return lax.axis_index("gx"), lax.axis_index("gy"), lax.axis_index("gz")


def at_offset(delta):
    return tuple(
        v if d % n == 0 else (v + (d % n)) & (n - 1) for v, d, n in zip(here(), delta, SIZES)
    )


def lanes(shape):
    return lax.broadcasted_iota(jnp.int32, shape, len(shape) - 1)


def sublanes(shape):
    return lax.broadcasted_iota(jnp.int32, shape, len(shape) - 2)


def pick_sum(choice, v):
    f32, bf16 = jnp.float32, jnp.bfloat16
    high = v.astype(bf16)
    rest = v - high.astype(f32)
    mid = rest.astype(bf16)
    low = (rest - mid.astype(f32)).astype(bf16)
    parts = jnp.dot(
        choice.astype(bf16), jnp.concatenate([high, mid, low], axis=1), preferred_element_type=f32
    )
    return parts[:, 0:128] + (parts[:, 128:256] + parts[:, 256:384])


def row_sum(v):
    total = v[0:8]
    for k in range(8, v.shape[0], 8):
        total = total + v[k : k + 8]
    for shift in (4, 2, 1):
        total = total + pltpu.roll(total, shift, 0)
    return total


def main_kernel(
    orb_hbm, pot_hbm, atom_hbm, points_hbm, count, beta_hbm, coup_hbm,
    image_ref, gram_ref,
    psi, pot, pts, beta, coup, atom,
    zb, hy, pk, msg, a2, row_own, rows16, onehot, spread,
    r1, pe, kr, stage, row_hub, ba, row_all, xrow, sent,
    lsem, hsend, hrecv, csend, crecv,
):
    f32 = jnp.float32
    loads = [
        pltpu.make_async_copy(orb_hbm, psi, lsem.at[0]),
        pltpu.make_async_copy(points_hbm.at[0, 0, 0], pts, lsem.at[1]),
        pltpu.make_async_copy(beta_hbm.at[0, 0, 0], beta, lsem.at[2]),
        pltpu.make_async_copy(atom_hbm, atom, lsem.at[3]),
        pltpu.make_async_copy(coup_hbm, coup, lsem.at[4]),
        pltpu.make_async_copy(pot_hbm, pot, lsem.at[5]),
    ]
    x, y, z = here()
    column = x * 8 + y
    is_hub = column == HUB

    def hub_of(d):
        return (0, HUB, (z + d) & 31)

    def member(c, d):
        return (c >> 3, c & 7, (z + d) & 31)

    barrier = pltpu.get_barrier_semaphore()

    def greet(device):
        pl.semaphore_signal(barrier, inc=1, device_id=device, device_id_type=MESH)

    for delta in reversed(HALOS[:4]):
        greet(at_offset(delta))
    for load in loads:
        load.start()
    for d in (-1, 1):
        greet(hub_of(d))

    @pl.when(jnp.logical_not(is_hub))
    def _():
        greet(hub_of(0))

    @pl.when(is_hub)
    def _():
        for d in (-1, 1):
            greet(hub_of(d))

        for c in MEMBERS:
            for d in SIDES:
                greet(member(c, d))
        for d in range(1, 32):
            greet(hub_of(d))

    def remote(src, dst, send, recv, device):
        return pltpu.make_async_remote_copy(
            src_ref=src, dst_ref=dst, send_sem=send, recv_sem=recv,
            device_id=device, device_id_type=MESH,
        )

    def wait_bytes(ref, sem):
        pltpu.make_async_copy(ref, ref, sem).wait()

    lane8, sub8 = lanes((8, 128)), sublanes((8, 128))
    loads[0].wait()

    pl.semaphore_wait(barrier, jnp.where(is_hub, 4 + 2 + 2 + 31 * 4, 4 + 3))
    halo_copies = [
        (psi.at[:, pl.ds(2, 2)], zb.at[0, :, pl.ds(2, 2)]),
        (psi.at[:, pl.ds(0, 2)], zb.at[1, :, pl.ds(0, 2)]),
        (psi.at[:, :, pl.ds(4, 4)], hy.at[:, :, pl.ds(4, 4)]),
        (psi.at[:, :, pl.ds(0, 4)], hy.at[:, :, pl.ds(0, 4)]),
        (psi.at[:, pl.ds(0, 2)], zb.at[0, :, pl.ds(0, 2)]),
        (psi.at[:, pl.ds(2, 2)], zb.at[1, :, pl.ds(2, 2)]),
    ]
    halos = [
        remote(src, dst, hsend.at[k], hrecv.at[k], at_offset(HALOS[k]))
        for k, (src, dst) in enumerate(halo_copies)
    ]
    for halo in halos[:4]:
        halo.start()

    packed = jnp.zeros((8, 128), f32)
    for n in range(4):
        for zz in range(4):
            g = n * 4 + zz
            moved = pltpu.roll(psi[n, zz], (4 + 8 * g) % 128, 1)
            packed = jnp.where(lane8 // 8 == g, moved, packed)
    pk[...] = packed

    @pl.when(jnp.logical_not(is_hub))
    def _():
        remote(pk, pe.at[column], csend.at[4], crecv.at[4], hub_of(0)).start()

    loads[1].wait()
    lo = [pts[8 * h : 8 * h + 8] & 127 for h in range(2)]
    hi = [pts[8 * h : 8 * h + 8] >> 7 for h in range(2)]
    gathered = [[jnp.zeros((8, 128), f32) for _ in range(2)] for _ in range(4)]
    for row in range(32):
        pick = [hi[h] == row for h in range(2)]
        for n in range(4):
            line = jnp.broadcast_to(psi[n, row // 8, row % 8 : row % 8 + 1], (8, 128))
            for h in range(2):
                got = jnp.take_along_axis(line, lo[h], axis=1)
                gathered[n][h] = jnp.where(pick[h], got, gathered[n][h])

    for load in loads[2:]:
        load.wait()
    slots = count[0, 0, 0]
    dir_of, back_of, kind_of = [], [], []
    for b in range(16):
        a = atom[0, 0, 0, b]
        owner = a // 3
        dx = ((owner & 3) - x + 1) & 3
        dy = (((owner >> 2) & 7) - y + 1) & 7
        dz = ((owner >> 5) - z + 1) & 31
        where = jnp.minimum(jnp.maximum(dz * 16 + dy * 3 + dx, 0), 47)
        back = jnp.minimum(jnp.maximum(dz * 24 + dy * 3 + dx + 8, 0), 71)
        dir_of.append(where)
        back_of.append(back)
        kind_of.append(a - owner * 3)
    dir_lane = jnp.full((48, 128), 63, jnp.int32)
    for b in range(16):
        used = jnp.where(b < slots, dir_of[b], 63)
        dir_lane = jnp.where(lanes((48, 128)) // 8 == b, used, dir_lane)
    select = (sublanes((48, 128)) == dir_lane).astype(f32)

    lane_n, lane_k, lane_p = lane8 // 32, (lane8 // 8) & 3, lane8 & 7
    blocks = []
    for b in range(16):
        block = jnp.zeros((8, 128), f32)
        for n in range(4):
            line = jnp.broadcast_to(gathered[n][b // 8][b % 8 : b % 8 + 1], (8, 128))
            part = jnp.sum(beta[b] * line, axis=1, keepdims=True)
            block = jnp.where(lane_n == n, part, block)
        keep = (lane_p == sub8) & (lane_k == kind_of[b])
        blocks.append(jnp.where(keep, block, 0.0))
    msg[...] = pick_sum(select, jnp.concatenate(blocks, axis=0))

    def send_rows(d):
        src, dst = msg.at[pl.ds(16 * (d + 1), 9)], r1.at[32 * (d + 1) + column, pl.ds(0, 9)]
        remote(src, dst, csend.at[0], crecv.at[0], hub_of(d)).start()

    send_rows(-1)
    send_rows(1)

    @pl.when(jnp.logical_not(is_hub))
    def _():
        send_rows(0)

    li, si = lanes((128, 128)), sublanes((128, 128))
    away = (li - si) & 127
    away = jnp.minimum(away, 128 - away)
    along_x = jnp.where(away == 0, 3.0 * KIN[0], 0.0)
    for o in range(1, 5):
        along_x = jnp.where(away == o, KIN[o], along_x)
    flat = psi[...].reshape(128, 128)
    base = jnp.dot(flat, along_x, precision=HIGH, preferred_element_type=f32)

    for b in range(16):
        line = jnp.broadcast_to(lo[b // 8][b % 8 : b % 8 + 1], (128, 128))
        onehot[:, pl.ds(b * 128, 128)] = (si == line).astype(jnp.bfloat16)

    halos[2].wait_recv()
    halos[3].wait_recv()
    sums = [None] * len(PAIRS)
    for zz in range(4):
        image = []
        for n in range(4):
            own, other = psi[n, zz], hy[n, zz]
            total = base[(n * 4 + zz) * 8 : (n * 4 + zz) * 8 + 8]
            for o in range(1, 5):
                before = pltpu.roll(jnp.where(sub8 < 8 - o, own, other), o, 0)
                after = pltpu.roll(jnp.where(sub8 >= o, own, other), 8 - o, 0)
                near = before + after
                if zz + o < 4:
                    near = near + psi[n, zz + o]
                if zz - o >= 0:
                    near = near + psi[n, zz - o]
                total = total + KIN[o] * near
            total = total + pot[zz] * own
            image.append(total)
            image_ref[n, zz] = total
        for k, (i, j) in enumerate(PAIRS):
            term = psi[i, zz] * image[j]
            sums[k] = term if sums[k] is None else sums[k] + term
    halos[0].wait_recv()
    halos[1].wait_recv()
    for zz in range(4):
        cross = []
        for n in range(4):
            total = KIN[4 - zz] * zb[1, n, 0]
            if zz >= 1:
                total = total + KIN[5 - zz] * zb[1, n, 1]
            for layer in (2, 3):
                if zz >= 2 and layer >= zz:
                    total = total + KIN[4 + zz - layer] * zb[0, n, layer]
            cross.append(total)
        for k, (i, j) in enumerate(PAIRS):
            sums[k] = sums[k] + (psi[i, zz] * cross[j] + psi[j, zz] * cross[i])
    local = jnp.zeros((8, 128), f32)
    for k, (i, j) in enumerate(PAIRS):
        total = jnp.sum(sums[k], axis=1, keepdims=True)
        local = jnp.where(lane8 == j * 32 + (j - i) * 8, total, local)
    row_own[...] = row_sum(local)

    @pl.when(jnp.logical_not(is_hub))
    def _():
        remote(
            row_own.at[pl.ds(0, 1)], kr.at[column, pl.ds(0, 1)], csend.at[5], crecv.at[5], hub_of(0)
        ).start()

    for halo in halos[4:]:
        halo.start()

    @pl.when(is_hub)
    def _():
        kr[HUB] = row_own[...]
        pe[HUB] = pk[...]
        r1[32 + HUB, pl.ds(0, 9)] = msg[pl.ds(16, 9)]
        sj, lj = si & 7, li & 7
        edge = jnp.zeros((128, 128), f32)
        for o in range(1, 5):
            left = (sj < 4) & (lj >= 4) & (lj - sj == o)
            right = (sj >= 4) & (lj < 4) & (sj - lj == o)
            edge = jnp.where((si // 8 == li // 8) & (left | right), KIN[o], edge)
        tiles = []
        for c in range(2):
            tile = jnp.concatenate([coup[c], jnp.zeros((8, 120), f32)], axis=1)
            for shift in (8, 16, 32, 64):
                tile = tile + pltpu.roll(tile, shift, 1)
            tiles.append(tile)
        couple = jnp.concatenate(
            [jnp.where(lane8 // 8 == r, tiles[0 if r % 4 == 0 else 1], 0.0) for r in range(16)],
            axis=0,
        )

        def reaches(box, c, r):
            third = (r * 11) >> 5
            tx = ((c >> 3) + (r - 3 * third) + 3) & 3
            ty = ((c & 7) + third + 7) & 7
            return ((r < 9) & (box == tx * 8 + ty)).astype(f32)

        col, box = lanes((32, 512)), sublanes((32, 512))
        collect = reaches(box, col >> 4, col & 15)
        row, box = sublanes((512, 32)), lanes((512, 32))
        spread_out = reaches(box, row >> 4, row & 15)

        wait_bytes(pe.at[pl.ds(0, 31)], crecv.at[4])
        edges = []
        for c in range(32):
            before, after = (c + 24) % 32, (c + 8) % 32
            edges.append(jnp.where(lane8 & 7 < 4, pe[before], pe[after]) - pe[c])
        change = jnp.dot(
            jnp.concatenate(edges, axis=0), edge, precision=HIGH, preferred_element_type=f32
        )
        outer = [jnp.zeros((8, 128), f32) for _ in range(4)]
        for c in range(32):
            part = change[8 * c : 8 * c + 8]
            stage[c, pl.ds(0, 8)] = part
            for s in range(4):
                outer[s] = outer[s] + (pltpu.roll(pe[c], 32 * s, 1) if s else pe[c]) * part

        wait_bytes(r1.at[pl.ds(0, 95), pl.ds(0, 9)], crecv.at[0])
        gathered_rows = (r1[pl.ds(0, 32)] + r1[pl.ds(64, 32)]) + r1[pl.ds(32, 32)]
        gathered_rows = jnp.where(sublanes((32, 16, 128)) < 9, gathered_rows, 0.0)
        coef = pick_sum(collect, gathered_rows.reshape(512, 128))
        applied = jnp.dot(coef, couple, precision=HIGH, preferred_element_type=f32)

        stage[:, pl.ds(8, 16)] = pick_sum(spread_out, applied).reshape(32, 16, 128)

        def hand_out(c, d):
            first, rows = (0, 17) if d == 0 else (8, 9)
            remote(
                stage.at[c, pl.ds(first, rows)], a2.at[pl.ds(24 * (1 - d) + first, rows)],
                csend.at[1], crecv.at[1], member(c, d),
            ).start()

        hand_out(HUB, -1)
        hand_out(HUB, 1)
        a2[pl.ds(24, 17)] = stage[HUB, pl.ds(0, 17)]
        for v in range(4):
            c8, a8 = coef[8 * v : 8 * v + 8], applied[8 * v : 8 * v + 8]
            for s in range(4):
                outer[s] = outer[s] + (pltpu.roll(c8, 32 * s, 1) if s else c8) * a8
        placed = jnp.zeros((8, 128), f32)
        for s in range(4):
            part = outer[s]
            part = (part + pltpu.roll(part, 120, 1)) + (pltpu.roll(part, 112, 1) + pltpu.roll(part, 104, 1))
            part = jnp.where(lane8 & 31 < 8, part, 0.0)
            placed = placed + (pltpu.roll(part, 8 * s, 1) if s else part)
        placed = row_sum(placed)
        wait_bytes(kr.at[pl.ds(0, 31), pl.ds(0, 1)], crecv.at[5])
        kinetic = kr[0]
        for c in range(1, 32):
            kinetic = kinetic + kr[c]
        row_hub[...] = placed + kinetic
        ba[pl.ds(31, 1)] = row_hub[pl.ds(0, 1)]
        for k, delta in enumerate(PLANE):
            remote(
                row_hub.at[pl.ds(0, 1)], ba.at[pl.ds(k, 1)], csend.at[2], crecv.at[2], at_offset(delta)
            ).start()
        for c in MEMBERS:
            for d in SIDES:
                hand_out(c, d)

    @pl.when(is_hub)
    def _():
        wait_bytes(a2.at[pl.ds(0, 18)], crecv.at[1])

    @pl.when(jnp.logical_not(is_hub))
    def _():
        wait_bytes(a2.at[pl.ds(0, 35)], crecv.at[1])

    halos[4].wait_recv()
    halos[5].wait_recv()
    for b in range(16):
        rows16[pl.ds(b, 1)] = a2[pl.ds(back_of[b], 1)]
    spots = []
    for h in range(2):
        kind = jnp.zeros((8, 128), jnp.int32)
        for b in range(8):
            kind = jnp.where(sub8 == b, kind_of[h * 8 + b], kind)
        spots.append(kind * 8 + lane_p)
    left = []
    for n in range(4):
        for h in range(2):
            got = jnp.take_along_axis(rows16[pl.ds(h * 8, 8)], spots[h] + 32 * n, axis=1)
            slot = sub8 + 8 * h
            left.append(jnp.where((lane8 // 8 == slot) & (slot < slots), got, 0.0))
    values = jnp.dot(
        jnp.concatenate(left, axis=0), beta[...].reshape(128, 128), precision=HIGH,
        preferred_element_type=f32,
    )
    high = values.astype(jnp.bfloat16).astype(f32)
    low = values - high
    for b in range(16):
        line = jnp.broadcast_to(hi[b // 8][b % 8 : b % 8 + 1], (32, 128))
        pick = sublanes((32, 128)) == line
        for part, source in enumerate((high, low)):
            for n in range(4):
                r = n * 16 + b
                piece = jnp.where(pick, jnp.broadcast_to(source[r : r + 1], (32, 128)), 0.0)
                spread[pl.ds(part * 128 + n * 32, 32), pl.ds(b * 128, 128)] = piece.astype(jnp.bfloat16)
    grid = lax.dot_general(
        spread[...], onehot[...], (((1,), (1,)), ((), ())), preferred_element_type=f32
    )
    at_edge = (lane8 < 4) | (lane8 >= 124)
    for n in range(4):
        for zz in range(4):
            g = n * 4 + zz
            moved = pltpu.roll(a2[pl.ds(24, 8)], (124 - 8 * g) % 128, 1)
            projected = grid[8 * g : 8 * g + 8] + grid[128 + 8 * g : 136 + 8 * g]
            total = image_ref[n, zz] + jnp.where(at_edge, moved, 0.0)
            for o in range(1, 5):
                if zz + o >= 4:
                    total = total + KIN[o] * zb[1, n, zz + o - 4]
                if zz - o < 0:
                    total = total + KIN[o] * zb[0, n, zz - o + 4]
            image_ref[n, zz] = total + projected

    @pl.when(is_hub)
    def _():
        wait_bytes(ba.at[pl.ds(0, 31)], crecv.at[2])
        row_all[...] = row_sum(ba[...])

        for c in MEMBERS:
            row = row_all.at[pl.ds(0, 1)]
            remote(row, xrow.at[pl.ds(0, 1)], csend.at[3], crecv.at[3], member(c, 0)).start()
        gram_ref[...] = row_all[...]
        wait_bytes(msg.at[pl.ds(0, 18)], csend.at[0])
        wait_bytes(sent.at[pl.ds(0, 95 * 9 + 31 * 8)], csend.at[1])
        wait_bytes(ba.at[pl.ds(0, 31)], csend.at[2])
        wait_bytes(kr.at[pl.ds(0, 31), pl.ds(0, 1)], csend.at[3])

    @pl.when(jnp.logical_not(is_hub))
    def _():
        wait_bytes(xrow.at[pl.ds(0, 1)], crecv.at[3])
        gram_ref[...] = jnp.broadcast_to(xrow[pl.ds(0, 1)], (8, 128))
        wait_bytes(msg.at[pl.ds(0, 27)], csend.at[0])
        wait_bytes(pk, csend.at[4])
        wait_bytes(row_own.at[pl.ds(0, 1)], csend.at[5])

    for halo in halos:
        halo.wait_send()


def residual_kernel(psi, image, gram, image_out, residual_out, residual, sem):
    copies = [pltpu.make_async_copy(image, image_out, sem.at[4])]
    copies[0].start()
    lane8 = lanes((8, 128))
    row = gram[...]
    weight = {}
    for i, j in PAIRS:
        group = j * 4 + (j - i)
        total = jnp.sum(jnp.where(lane8 // 8 == group, row, 0.0), axis=1, keepdims=True)
        total = jnp.broadcast_to(total, (8, 128)) * (1.0 / GRID_TOTAL)
        weight[i, j] = weight[j, i] = total
    for j in range(4):
        for z in range(4):
            total = image[j, z]
            for i in range(4):
                total = total - weight[i, j] * psi[i, z]
            residual[j, z] = total
        copies.append(pltpu.make_async_copy(residual.at[j], residual_out.at[j], sem.at[j]))
        copies[-1].start()
    for copy in copies:
        copy.wait()


def on_device(orbitals, potential, block_atom, block_points, block_count, projector_values, coupling):
    f32, i32 = jnp.float32, jnp.int32
    hbm = pl.BlockSpec(memory_space=pl.ANY)
    vmem = pl.BlockSpec(memory_space=pltpu.VMEM)
    field = jax.ShapeDtypeStruct((4, 4, 8, 128), f32)
    held = [
        pltpu.with_memory_space_constraint(v, pltpu.HBM)
        for v in (orbitals, potential, block_atom, block_points, projector_values, coupling)
    ]
    held.insert(4, block_count)
    image, gram = pl.pallas_call(
        main_kernel,
        out_shape=(pltpu.VMEM((4, 4, 8, 128), f32), pltpu.VMEM((8, 128), f32)),
        in_specs=[hbm] * 4 + [pl.BlockSpec(memory_space=pltpu.SMEM)] + [hbm] * 2,
        out_specs=(vmem, vmem),
        scratch_shapes=[
            pltpu.VMEM((4, 4, 8, 128), f32),
            pltpu.VMEM((4, 8, 128), f32),
            pltpu.VMEM((16, 128), i32),
            pltpu.VMEM((16, 8, 128), f32),
            pltpu.VMEM((2, 8, 8), f32),
            pltpu.SMEM((1, 1, 1, 16), i32),
            pltpu.VMEM((2, 4, 4, 8, 128), f32),
            pltpu.VMEM((4, 4, 8, 128), f32),
            pltpu.VMEM((8, 128), f32),
            pltpu.VMEM((48, 128), f32),
            pltpu.VMEM((72, 128), f32),
            pltpu.VMEM((8, 128), f32),
            pltpu.VMEM((16, 128), f32),
            pltpu.VMEM((128, 2048), jnp.bfloat16),
            pltpu.VMEM((256, 2048), jnp.bfloat16),
            pltpu.VMEM((96, 16, 128), f32),
            pltpu.VMEM((32, 8, 128), f32),
            pltpu.VMEM((32, 8, 128), f32),
            pltpu.VMEM((32, 24, 128), f32),
            pltpu.VMEM((8, 128), f32),
            pltpu.VMEM((32, 128), f32),
            pltpu.VMEM((8, 128), f32),
            pltpu.VMEM((8, 128), f32),
            pltpu.VMEM((1104, 128), f32),
            pltpu.SemaphoreType.DMA((6,)),
            pltpu.SemaphoreType.DMA((6,)),
            pltpu.SemaphoreType.DMA((6,)),
            pltpu.SemaphoreType.DMA((6,)),
            pltpu.SemaphoreType.DMA((6,)),
        ],
        compiler_params=pltpu.CompilerParams(
            collective_id=0, has_side_effects=True, vmem_limit_bytes=24 * 1024 * 1024
        ),
    )(*held)
    return pl.pallas_call(
        residual_kernel,
        out_shape=(field, field),
        in_specs=[vmem] * 3,
        out_specs=(hbm, hbm),
        scratch_shapes=[pltpu.VMEM((4, 4, 8, 128), f32), pltpu.SemaphoreType.DMA((5,))],
        compiler_params=pltpu.CompilerParams(vmem_limit_bytes=16 * 1024 * 1024),
    )(orbitals, image, gram)


def solution(mesh):
    return jax.shard_map(
        on_device,
        mesh=mesh,
        in_specs=(
            P(None, "gz", "gy", "gx"),
            P("gz", "gy", "gx"),
            P("gz", "gy", "gx", None),
            P("gz", "gy", "gx", None, None),
            P("gz", "gy", "gx"),
            P("gz", "gy", "gx", None, None, None),
            P(),
        ),
        out_specs=(P(None, "gz", "gy", "gx"), P(None, "gz", "gy", "gx")),
        check_vma=False,
    )
```
